512 devices in a mesh: band: 16 (over x_lo, y), fft: 32 (over z, x_hi, core).
Axes of the slice: x: 4 (x_hi: 2, x_lo: 2; x = x_hi * 2 + x_lo), y: 8, z: 8, core: 2. Of those that a mesh axis runs over, the one named last changes fastest.
Arguments:
- orbitals: float32 [32, 128, 128, 128], P('band', 'fft'), may hold values from -2 to 2
- owner: int32 [4], replicated, may hold values from 0 to 15
- occupied: int32 [16, 2], replicated, may hold values from 0 to 1, as said below
Outputs:
- exchange: float32 [32, 128, 128, 128], P('band', 'fft')
The draws below stay inside these ranges and needn't reach their ends.
Inputs may be any that keep to these rules, and one draw needn't show every extreme that they name: `occupied`: each row names 2 different local orbitals of its band group.
All inputs are finite; a program needn't handle non-finite values.
Results may differ from the reference program's by a relative error of at most 0.0001.
Values sent between devices are 32-bit elements; how exact they have to be, the bound alone decides.
No kernel may reach another device: no remote copies, remote signals or barrier semaphores. Data moves between devices by JAX's collectives and lax.ppermute only.
A program may use at most 64 MiB of HBM per device.

```python
import math
import jax
import jax.numpy as jnp
from jax import lax

NG = 128
NB_DEV = 2
SEND = 2
NBANDS = 32
N_BAND = 16


def draw_occupied(key, part):
    key = jax.random.fold_in(key, 7)
    order_key, rows_key = jax.random.split(key)
    shuffled = jax.random.permutation(order_key, NB_DEV).astype(jnp.int32)
    row_order = jax.random.permutation(rows_key, N_BAND).astype(jnp.int32)
    starts = row_order[:, None] * SEND + jnp.arange(SEND, dtype=jnp.int32)[None, :]
    positions = starts % NB_DEV
    return jnp.take(shuffled, positions).astype(jnp.int32)


def draw_orbitals(key, part):
    key = jax.random.fold_in(key, 11)
    keys = jax.random.split(key, 4)
    couples = NBANDS // 2
    flip = jax.random.randint(keys[0], (couples,), 0, 2).astype(jnp.int32)
    position = jnp.arange(NBANDS, dtype=jnp.int32)
    transported_state = (position % 2 == jnp.repeat(flip, 2)).astype(jnp.float32)[:, None, None, None]
    phase = jax.random.uniform(keys[1], (NBANDS, 1, NG, NG), jnp.float32, -math.pi, math.pi)
    slope = jax.random.randint(keys[2], (NBANDS, 1, NG, NG), -2, 3).astype(jnp.float32)
    cells = jnp.arange(NG, dtype=jnp.int32)
    along = cells.astype(jnp.float32)[None, :, None, None]
    alternating_factor = (1.0 - 2.0 * (cells % 2).astype(jnp.float32))[None, :, None, None]
    modulating_harmonic = transported_state * alternating_factor + (1.0 - transported_state)
    wave = jnp.cos(phase + 2.0 * math.pi / NG * slope * along)
    sharp = 2.5
    stochastic_jitter = 0.2 * jnp.clip(jax.random.normal(keys[3], (NBANDS, NG, NG, NG), jnp.float32), -2.5, 2.5)
    lattice_layout = jnp.tanh(sharp * wave) / math.tanh(sharp)
    return (1.5 * modulating_harmonic * lattice_layout + stochastic_jitter).astype(jnp.float32)


def set_ends(result, stream_key, smallest, largest):
    shape = result.shape
    place = [jax.random.randint(jax.random.fold_in(stream_key, axis), (), 0, shape[axis]) for axis in range(len(shape))]
    result = result.at[tuple(place)].set(smallest)
    longest = shape.index(max(shape))
    place[longest] = (place[longest] + 1) % shape[longest]
    return result.at[tuple(place)].set(largest)


def setup_inputs(seed: int = 0) -> dict:
    key_of = jax.random.split(jax.random.key(seed), 4)
    orbitals = draw_orbitals(jax.random.fold_in(key_of[3], 71), 0)
    owner = set_ends(jax.random.randint(key_of[1], (4,), 0, N_BAND), jax.random.fold_in(key_of[1], 1), 0, N_BAND - 1).astype(jnp.int32)
    occupied = draw_occupied(jax.random.fold_in(key_of[3], 71), 0)
    return {"orbitals": orbitals, "owner": owner, "occupied": occupied}


SCREEN = 0.025
FRACTION = 0.25


def kernel_grid():
    spatial_tempo = jnp.arange(NG, dtype=jnp.int32)
    signed_values = jnp.where(spatial_tempo <= NG // 2, spatial_tempo, spatial_tempo - NG).astype(jnp.float32)
    wave = signed_values * (2.0 * math.pi / NG)
    g_square = wave[:, None, None] ** 2 + wave[None, :, None] ** 2 + wave[None, None, :] ** 2
    return 4.0 * math.pi / (g_square + SCREEN)


def reference(orbitals, owner, occupied):
    leader = owner[0]
    chosen_rows = (leader * NB_DEV + occupied[leader]).astype(jnp.int32)
    received = jnp.take(orbitals, chosen_rows, axis=0)
    kernel = kernel_grid()

    def exchange_one(orbital):
        accumulated = jnp.zeros_like(orbital)
        for position in range(SEND):
            density = orbital * received[position]
            coulomb_kernel = jnp.real(jnp.fft.ifftn(kernel * jnp.fft.fftn(density)))
            accumulated = accumulated + coulomb_kernel * received[position]
        return -FRACTION * accumulated

    return lax.map(exchange_one, orbitals)
```

```python
import math

import jax
import jax.numpy as jnp
import numpy as np
from jax import lax
from jax.experimental import pallas as pl
from jax.experimental.pallas import tpu as pltpu
from jax.sharding import PartitionSpec as P

SCREEN = 0.025
FRACTION = 0.25
LANES = 128
VMEM_LIMIT = 40 * 1024 * 1024


def wave_matrix(length):
    indices = np.arange(length)
    angles = (indices[:, None] * indices[None, :] % length) * (2.0 * math.pi / length)
    cosine, sine = np.cos(angles), np.sin(angles)
    return np.block([[cosine, sine], [-sine, cosine]]).astype(np.float32)


def split(value):
    high = value.astype(jnp.bfloat16)
    low = (value - high.astype(jnp.float32)).astype(jnp.bfloat16)
    return high, low


def dot(left, right):
    return jnp.dot(left, right, preferred_element_type=jnp.float32)


def left_product(matrix, value):
    high, low = split(value)
    return dot(matrix[0], high) + (dot(matrix[0], low) + dot(matrix[1], high))


def right_product(value, matrix):
    high, low = split(value)
    return dot(high, matrix[0]) + (dot(low, matrix[0]) + dot(high, matrix[1]))


def forward_kernel(order, orbitals, received, left, right, out):
    planes, length = orbitals.shape[1], orbitals.shape[2]
    partners = received.shape[0]
    stride = partners * 2 * planes
    left, right = split(left[...]), split(right[...])
    for j in range(partners):
        for p in range(planes):
            partner = received[order[j], p]
            field = jnp.concatenate([orbitals[0, p] * partner, orbitals[1, p] * partner], axis=1)
            along_z = right_product(field, right)
            stacked = jnp.concatenate([along_z[:, :length], along_z[:, length:]], axis=0)
            both = left_product(left, stacked)
            for c in range(2):
                row = (j * 2 + c) * planes + p
                out[pl.ds(row, length, stride=stride), :] = both[c * length : (c + 1) * length]


def signed_wave(index, length):
    signed = jnp.where(index <= length // 2, index, index - length)
    return signed.astype(jnp.float32) * (2.0 * math.pi / length)


def middle_kernel(first, field, forward, backward, out):
    sources, rows, partners, parts, lanes = field.shape
    planes = parts // 2
    length = sources * planes
    size = sources * parts
    row = lax.broadcasted_iota(jnp.int32, (size, lanes), 0)
    x_index = (row // parts) * planes + row % planes
    wave_x = signed_wave(x_index, length)
    wave_z = signed_wave(lax.broadcasted_iota(jnp.int32, (size, lanes), 1), length)
    flat = wave_x * wave_x + wave_z * wave_z + SCREEN
    forward, backward = split(forward[...]), split(backward[...])
    factor = -FRACTION * 4.0 * math.pi / float(length**3)
    for k in range(rows):
        wave_y = signed_wave(first[0] + k, length)
        kernel = factor / (flat + wave_y * wave_y)
        for j in range(partners):
            value = field[:, k, j].reshape(size, lanes)
            value = left_product(forward, value) * kernel
            value = left_product(backward, value)
            out[:, k, j] = value.reshape(sources, parts, lanes)


def backward_kernel(order, field, received, left, right, out):
    planes, length = received.shape[1], received.shape[2]
    partners = received.shape[0]
    stride = partners * 2 * planes
    left, right = split(left[...]), split(right[...])
    for p in range(planes):
        totals = None
        for j in range(partners):
            partner = received[order[j], p]
            stacked = jnp.concatenate(
                [field[pl.ds((j * 2 + c) * planes + p, length, stride=stride), :] for c in range(2)],
                axis=0,
            )
            along_y = left_product(left, stacked)
            wide = jnp.concatenate([along_y[:length], along_y[length:]], axis=1)
            both = right_product(wide, right)
            terms = [both[:, :length] * partner, both[:, length:] * partner]
            totals = terms if totals is None else [a + b for a, b in zip(totals, terms)]
        for c in range(2):
            out[c, p] = totals[c]


def smem():
    return pl.BlockSpec(memory_space=pltpu.SMEM)


def vmem():
    return pl.BlockSpec(memory_space=pltpu.VMEM)


def call(kernel, shape, specs, flops, name):
    return pl.pallas_call(
        kernel,
        out_shape=jax.ShapeDtypeStruct(shape, jnp.float32),
        in_specs=specs,
        out_specs=vmem(),
        compiler_params=pltpu.CompilerParams(vmem_limit_bytes=VMEM_LIMIT),
        cost_estimate=pl.CostEstimate(flops=flops, bytes_accessed=4 << 20, transcendentals=0),
        name=name,
    )


def body(orbitals, owner, occupied):
    bands, planes, length, _ = orbitals.shape
    groups = lax.axis_size("band")
    columns = lax.axis_size("fft")
    rows = length // columns
    partners = occupied.shape[1]
    leader = owner[0]
    order = lax.dynamic_index_in_dim(occupied, leader, 0, keepdims=False)

    pieces = orbitals.reshape(groups, -1, LANES)
    with jax.named_scope("scatter"):
        pieces = lax.all_to_all(pieces, "band", 0, 0, tiled=True)
        mine = lax.dynamic_index_in_dim(pieces, leader, 0, keepdims=True)
        mine = jnp.broadcast_to(mine, pieces.shape)
    with jax.named_scope("gather"):
        received = lax.all_to_all(mine, "band", 0, 0, tiled=True).reshape(orbitals.shape)

    matrix = wave_matrix(length)
    left, right = matrix, matrix.T.copy()
    x_index = np.arange(length).reshape(columns, 1, planes) + np.array([0, length])[None, :, None]
    x_index = x_index.reshape(-1)
    mixed = matrix[np.ix_(x_index, x_index)]
    x_forward, x_backward = mixed, mixed.T.copy()

    size = 3 * 2 * 2 * length * 2 * length * partners * planes * length * 2
    total = length * partners * 2 * planes
    spectrum = call(
        forward_kernel, (total, LANES), [smem()] + [vmem()] * 4, size, "forward_zy"
    )(order, orbitals, received, left, right)
    with jax.named_scope("to_columns"):
        spectrum = lax.all_to_all(
            spectrum.reshape(columns, rows * partners * 2 * planes, LANES), "fft", 0, 0, tiled=True
        )
    first = (lax.axis_index("fft") * rows).astype(jnp.int32).reshape(1)
    shape = (columns, rows, partners, 2 * planes, LANES)
    spectrum = call(
        middle_kernel, shape, [smem()] + [vmem()] * 3, size, "solve_x"
    )(first, spectrum.reshape(shape), x_forward, x_backward)
    with jax.named_scope("to_planes"):
        spectrum = lax.all_to_all(
            spectrum.reshape(columns, rows * partners * 2 * planes, LANES), "fft", 0, 0, tiled=True
        )
    return call(
        backward_kernel, orbitals.shape, [smem()] + [vmem()] * 4, size, "backward_yz"
    )(order, spectrum.reshape(total, LANES), received, right, left)


def solution(mesh):
    return jax.shard_map(
        body,
        mesh=mesh,
        in_specs=(P("band", "fft", None, None), P(), P()),
        out_specs=P("band", "fft", None, None),
        check_vma=False,
    )
```

```python
import math

import jax
import jax.numpy as jnp
import numpy as np
from jax import lax
from jax.experimental import pallas as pl
from jax.experimental.pallas import tpu as pltpu
from jax.sharding import PartitionSpec as P

SCREEN = 0.025
FRACTION = 0.25
LANES = 128
BATCH = 2
VMEM_LIMIT = 40 * 1024 * 1024


def wave_matrix(length):
    indices = np.arange(length)
    angles = (indices[:, None] * indices[None, :] % length) * (2.0 * math.pi / length)
    cosine, sine = np.cos(angles), np.sin(angles)
    return np.block([[cosine, sine], [-sine, cosine]]).astype(np.float32)


def split(value):
    high = value.astype(jnp.bfloat16)
    low = (value - high.astype(jnp.float32)).astype(jnp.bfloat16)
    return high, low


def dot(left, right):
    return jnp.dot(left, right, preferred_element_type=jnp.float32)


def left_product(matrix, value):
    high, low = split(value)
    return dot(matrix[0], high) + (dot(matrix[0], low) + dot(matrix[1], high))


def right_product(value, matrix):
    high, low = split(value)
    return dot(high, matrix[0]) + (dot(low, matrix[0]) + dot(high, matrix[1]))


def spread_kernel(leader, pieces, out):
    piece = pieces[leader[0]]
    for k in range(out.shape[0]):
        out[k] = piece


def tile(value, row, column, size):
    return value[row * size : (row + 1) * size, column * size : (column + 1) * size]


def forward_kernel(order, orbitals, received, left, right, out):
    planes, length = orbitals.shape[1], orbitals.shape[2]
    partners = received.shape[0]
    stride = partners * 2 * planes
    left, right = split(left[...]), split(right[...])
    for j in range(partners):
        for first in range(0, planes, BATCH):
            group = range(first, first + BATCH)
            fields = []
            for p in group:
                partner = received[order[j], p]
                fields.append(jnp.concatenate([orbitals[c, p] * partner for c in range(2)], axis=1))
            along_z = right_product(jnp.concatenate(fields, axis=0), right)
            blocks = [
                jnp.concatenate([tile(along_z, k, c, length) for k in range(BATCH)], axis=1)
                for c in range(2)
            ]
            both = left_product(left, jnp.concatenate(blocks, axis=0))
            for k, p in enumerate(group):
                for c in range(2):
                    row = (j * 2 + c) * planes + p
                    out[pl.ds(row, length, stride=stride), :] = tile(both, c, k, length)


def signed_wave(index, length):
    signed = jnp.where(index <= length // 2, index, index - length)
    return signed.astype(jnp.float32) * (2.0 * math.pi / length)


def middle_kernel(first, field, forward, backward, out):
    sources, rows, partners, parts, lanes = field.shape
    planes = parts // 2
    length = sources * planes
    size = sources * parts
    row = lax.broadcasted_iota(jnp.int32, (size, lanes), 0)
    x_index = (row // parts) * planes + row % planes
    wave_x = signed_wave(x_index, length)
    wave_z = signed_wave(lax.broadcasted_iota(jnp.int32, (size, lanes), 1), length)
    flat = wave_x * wave_x + wave_z * wave_z + SCREEN
    forward, backward = split(forward[...]), split(backward[...])
    factor = -FRACTION * 4.0 * math.pi / float(length**3)
    kernels = []
    for k in range(rows):
        wave_y = signed_wave(first[0] + k, length)
        kernels += [factor / (flat + wave_y * wave_y)] * partners
    items = [(k, j) for k in range(rows) for j in range(partners)]
    value = jnp.concatenate([field[:, k, j].reshape(size, lanes) for k, j in items], axis=1)
    value = left_product(forward, value) * jnp.concatenate(kernels, axis=1)
    value = left_product(backward, value)
    for n, (k, j) in enumerate(items):
        out[:, k, j] = value[:, n * lanes : (n + 1) * lanes].reshape(sources, parts, lanes)


def backward_kernel(order, field, received, left, right, out, result, done):
    planes, length = received.shape[1], received.shape[2]
    partners = received.shape[0]
    stride = partners * 2 * planes
    left, right = split(left[...]), split(right[...])
    copies = []
    for p in range(planes):
        blocks = []
        for c in range(2):
            rows = [pl.ds((j * 2 + c) * planes + p, length, stride=stride) for j in range(partners)]
            blocks.append(jnp.concatenate([field[row, :] for row in rows], axis=1))
        along_y = left_product(left, jnp.concatenate(blocks, axis=0))
        wide = [
            jnp.concatenate([tile(along_y, c, j, length) for c in range(2)], axis=1)
            for j in range(partners)
        ]
        both = right_product(jnp.concatenate(wide, axis=0), right)
        for c in range(2):
            result[c, p] = sum(
                tile(both, j, c, length) * received[order[j], p] for j in range(partners)
            )
            copies.append(pltpu.make_async_copy(result.at[c, p], out.at[c, p], done.at[c, p]))
            copies[-1].start()
    for copy in copies:
        copy.wait()


def smem():
    return pl.BlockSpec(memory_space=pltpu.SMEM)


def vmem():
    return pl.BlockSpec(memory_space=pltpu.VMEM)


def call(kernel, shape, specs, flops, name, **options):
    options.setdefault("out_specs", vmem())
    return pl.pallas_call(
        kernel,
        out_shape=jax.ShapeDtypeStruct(shape, jnp.float32),
        in_specs=specs,
        compiler_params=pltpu.CompilerParams(vmem_limit_bytes=VMEM_LIMIT),
        cost_estimate=pl.CostEstimate(flops=flops, bytes_accessed=4 << 20, transcendentals=0),
        name=name,
        **options,
    )


def body(orbitals, owner, occupied):
    bands, planes, length, _ = orbitals.shape
    groups = lax.axis_size("band")
    columns = lax.axis_size("fft")
    rows = length // columns
    partners = occupied.shape[1]
    leader = owner[0]
    order = lax.dynamic_index_in_dim(occupied, leader, 0, keepdims=False)

    pieces = orbitals.reshape(groups, -1, LANES)
    with jax.named_scope("scatter"):
        pieces = lax.all_to_all(pieces, "band", 0, 0, tiled=True)
        mine = call(spread_kernel, pieces.shape, [smem(), vmem()], 0, "spread")(
            leader.reshape(1), pieces
        )
    with jax.named_scope("gather"):
        received = lax.all_to_all(mine, "band", 0, 0, tiled=True).reshape(orbitals.shape)

    matrix = wave_matrix(length)
    left, right = matrix, matrix.T.copy()
    x_index = np.arange(length).reshape(columns, 1, planes) + np.array([0, length])[None, :, None]
    x_index = x_index.reshape(-1)
    mixed = matrix[np.ix_(x_index, x_index)]
    x_forward, x_backward = mixed, mixed.T.copy()

    size = 3 * 2 * 2 * length * 2 * length * partners * planes * length * 2
    total = length * partners * 2 * planes
    spectrum = call(
        forward_kernel, (total, LANES), [smem()] + [vmem()] * 4, size, "forward_zy"
    )(order, orbitals, received, left, right)
    with jax.named_scope("to_columns"):
        spectrum = lax.all_to_all(
            spectrum.reshape(columns, rows * partners * 2 * planes, LANES), "fft", 0, 0, tiled=True
        )
    first = (lax.axis_index("fft") * rows).astype(jnp.int32).reshape(1)
    shape = (columns, rows, partners, 2 * planes, LANES)
    spectrum = call(
        middle_kernel, shape, [smem()] + [vmem()] * 3, size, "solve_x"
    )(first, spectrum.reshape(shape), x_forward, x_backward)
    with jax.named_scope("to_planes"):
        spectrum = lax.all_to_all(
            spectrum.reshape(columns, rows * partners * 2 * planes, LANES), "fft", 0, 0, tiled=True
        )
    return call(
        backward_kernel,
        orbitals.shape,
        [smem()] + [vmem()] * 4,
        size,
        "backward_yz",
        out_specs=pl.BlockSpec(memory_space=pl.ANY),
        scratch_shapes=[
            pltpu.VMEM(orbitals.shape, jnp.float32),
            pltpu.SemaphoreType.DMA((bands, planes)),
        ],
    )(order, spectrum.reshape(total, LANES), received, right, left)


def solution(mesh):
    return jax.shard_map(
        body,
        mesh=mesh,
        in_specs=(P("band", "fft", None, None), P(), P()),
        out_specs=P("band", "fft", None, None),
        check_vma=False,
    )
```

```python
import math

import jax
import jax.numpy as jnp
import numpy as np
from jax import lax
from jax.experimental import pallas as pl
from jax.experimental.pallas import tpu as pltpu
from jax.sharding import PartitionSpec as P

SCREEN = 0.025
FRACTION = 0.25
LANES = 128
BATCH = 2
VMEM_LIMIT = 40 * 1024 * 1024


def wave_matrix(length):
    indices = np.arange(length)
    angles = (indices[:, None] * indices[None, :] % length) * (2.0 * math.pi / length)
    cosine, sine = np.cos(angles), np.sin(angles)
    return np.block([[cosine, sine], [-sine, cosine]]).astype(np.float32)


def split(value):
    high = value.astype(jnp.bfloat16)
    low = (value - high.astype(jnp.float32)).astype(jnp.bfloat16)
    return high, low


def dot(left, right):
    return jnp.dot(left, right, preferred_element_type=jnp.float32)


def left_product(matrix, value):
    high, low = split(value)
    return dot(matrix[0], high) + (dot(matrix[0], low) + dot(matrix[1], high))


def right_product(value, matrix):
    high, low = split(value)
    return dot(high, matrix[0]) + (dot(low, matrix[0]) + dot(high, matrix[1]))


def spread_kernel(owner, pieces, out):
    piece = pieces[owner[0]]
    for k in range(out.shape[0]):
        out[k] = piece


def tile(value, row, column, size):
    return value[row * size : (row + 1) * size, column * size : (column + 1) * size]


def forward_kernel(owner, occupied, orbitals, received, left, right, out):
    planes, length = orbitals.shape[1], orbitals.shape[2]
    partners = received.shape[0]
    stride = partners * 2 * planes
    left, right = split(left[...]), split(right[...])
    for j in range(partners):
        for first in range(0, planes, BATCH):
            group = range(first, first + BATCH)
            fields = []
            for p in group:
                partner = received[occupied[j, owner[0]], p]
                fields.append(jnp.concatenate([orbitals[c, p] * partner for c in range(2)], axis=1))
            along_z = right_product(jnp.concatenate(fields, axis=0), right)
            blocks = [
                jnp.concatenate([tile(along_z, k, c, length) for k in range(BATCH)], axis=1)
                for c in range(2)
            ]
            both = left_product(left, jnp.concatenate(blocks, axis=0))
            for k, p in enumerate(group):
                for c in range(2):
                    row = (j * 2 + c) * planes + p
                    out[pl.ds(row, length, stride=stride), :] = tile(both, c, k, length)


def signed_wave(index, length):
    signed = jnp.where(index <= length // 2, index, index - length)
    return signed.astype(jnp.float32) * (2.0 * math.pi / length)


def middle_kernel(field, forward, backward, out):
    sources, rows, partners, parts, lanes = field.shape
    planes = parts // 2
    length = sources * planes
    size = sources * parts
    row = lax.broadcasted_iota(jnp.int32, (size, lanes), 0)
    x_index = (row // parts) * planes + row % planes
    wave_x = signed_wave(x_index, length)
    wave_z = signed_wave(lax.broadcasted_iota(jnp.int32, (size, lanes), 1), length)
    flat = wave_x * wave_x + wave_z * wave_z + SCREEN
    forward, backward = split(forward[...]), split(backward[...])
    factor = -FRACTION * 4.0 * math.pi / float(length**3)
    kernels = []
    for k in range(rows):
        wave_y = signed_wave(lax.axis_index("fft") * rows + k, length)
        kernels += [factor / (flat + wave_y * wave_y)] * partners
    items = [(k, j) for k in range(rows) for j in range(partners)]
    value = jnp.concatenate([field[:, k, j].reshape(size, lanes) for k, j in items], axis=1)
    value = left_product(forward, value) * jnp.concatenate(kernels, axis=1)
    value = left_product(backward, value)
    for n, (k, j) in enumerate(items):
        out[:, k, j] = value[:, n * lanes : (n + 1) * lanes].reshape(sources, parts, lanes)


def backward_kernel(owner, occupied, field, received, left, right, out, result, done):
    planes, length = received.shape[1], received.shape[2]
    partners = received.shape[0]
    stride = partners * 2 * planes
    left, right = split(left[...]), split(right[...])
    copies = []
    for p in range(planes):
        blocks = []
        for c in range(2):
            rows = [pl.ds((j * 2 + c) * planes + p, length, stride=stride) for j in range(partners)]
            blocks.append(jnp.concatenate([field[row, :] for row in rows], axis=1))
        along_y = left_product(left, jnp.concatenate(blocks, axis=0))
        wide = [
            jnp.concatenate([tile(along_y, c, j, length) for c in range(2)], axis=1)
            for j in range(partners)
        ]
        both = right_product(jnp.concatenate(wide, axis=0), right)
        for c in range(2):
            result[c, p] = sum(
                tile(both, j, c, length) * received[occupied[j, owner[0]], p] for j in range(partners)
            )
            copies.append(pltpu.make_async_copy(result.at[c, p], out.at[c, p], done.at[c, p]))
            copies[-1].start()
    for copy in copies:
        copy.wait()


def smem():
    return pl.BlockSpec(memory_space=pltpu.SMEM)


def vmem():
    return pl.BlockSpec(memory_space=pltpu.VMEM)


def call(kernel, shape, specs, flops, name, **options):
    options.setdefault("out_specs", vmem())
    return pl.pallas_call(
        kernel,
        out_shape=jax.ShapeDtypeStruct(shape, jnp.float32),
        in_specs=specs,
        compiler_params=pltpu.CompilerParams(vmem_limit_bytes=VMEM_LIMIT),
        cost_estimate=pl.CostEstimate(flops=flops, bytes_accessed=4 << 20, transcendentals=0),
        name=name,
        **options,
    )


def body(orbitals, owner, occupied):
    bands, planes, length, _ = orbitals.shape
    groups = lax.axis_size("band")
    columns = lax.axis_size("fft")
    rows = length // columns
    partners = occupied.shape[1]

    pieces = orbitals.reshape(groups, -1, LANES)
    with jax.named_scope("scatter"):
        pieces = lax.all_to_all(pieces, "band", 0, 0, tiled=True)
        mine = call(spread_kernel, pieces.shape, [smem(), vmem()], 0, "spread")(
            owner, pieces
        )
    with jax.named_scope("gather"):
        received = lax.all_to_all(mine, "band", 0, 0, tiled=True).reshape(orbitals.shape)

    matrix = wave_matrix(length)
    left, right = matrix, matrix.T.copy()
    x_index = np.arange(length).reshape(columns, 1, planes) + np.array([0, length])[None, :, None]
    x_index = x_index.reshape(-1)
    mixed = matrix[np.ix_(x_index, x_index)]
    x_forward, x_backward = mixed, mixed.T.copy()

    size = 3 * 2 * 2 * length * 2 * length * partners * planes * length * 2
    total = length * partners * 2 * planes
    spectrum = call(
        forward_kernel, (total, LANES), [smem()] * 2 + [vmem()] * 4, size, "forward_zy"
    )(owner, occupied.T, orbitals, received, left, right)
    with jax.named_scope("to_columns"):
        spectrum = lax.all_to_all(
            spectrum.reshape(columns, rows * partners * 2 * planes, LANES), "fft", 0, 0, tiled=True
        )
    shape = (columns, rows, partners, 2 * planes, LANES)
    spectrum = call(
        middle_kernel, shape, [vmem()] * 3, size, "solve_x"
    )(spectrum.reshape(shape), x_forward, x_backward)
    with jax.named_scope("to_planes"):
        spectrum = lax.all_to_all(
            spectrum.reshape(columns, rows * partners * 2 * planes, LANES), "fft", 0, 0, tiled=True
        )
    return call(
        backward_kernel,
        orbitals.shape,
        [smem()] * 2 + [vmem()] * 4,
        size,
        "backward_yz",
        out_specs=pl.BlockSpec(memory_space=pl.ANY),
        scratch_shapes=[
            pltpu.VMEM(orbitals.shape, jnp.float32),
            pltpu.SemaphoreType.DMA((bands, planes)),
        ],
    )(owner, occupied.T, spectrum.reshape(total, LANES), received, right, left)


def solution(mesh):
    return jax.shard_map(
        body,
        mesh=mesh,
        in_specs=(P("band", "fft", None, None), P(), P()),
        out_specs=P("band", "fft", None, None),
        check_vma=False,
    )
```

```python
import math

import jax
import jax.numpy as jnp
import numpy as np
from jax import lax
from jax.experimental import pallas as pl
from jax.experimental.pallas import tpu as pltpu
from jax.sharding import PartitionSpec as P

SCREEN = 0.025
FRACTION = 0.25
LANES = 128
BATCH = 2
RING = 8
VMEM_LIMIT = 40 * 1024 * 1024


def wave_matrix(length):
    indices = np.arange(length)
    angles = (indices[:, None] * indices[None, :] % length) * (2.0 * math.pi / length)
    cosine, sine = np.cos(angles), np.sin(angles)
    return np.block([[cosine, sine], [-sine, cosine]]).astype(np.float32)


def split(value):
    high = value.astype(jnp.bfloat16)
    low = (value - high.astype(jnp.float32)).astype(jnp.bfloat16)
    return high, low


def dot(left, right):
    return jnp.dot(left, right, preferred_element_type=jnp.float32)


def left_product(matrix, value):
    high, low = split(value)
    return dot(matrix[0], high) + (dot(matrix[0], low) + dot(matrix[1], high))


def right_product(value, matrix):
    high, low = split(value)
    return dot(high, matrix[0]) + (dot(low, matrix[0]) + dot(high, matrix[1]))


def spread_kernel(owner, occupied, pieces, out):
    piece = pieces[owner[0]]
    for k in range(out.shape[0]):
        out[k] = piece


def tile(value, row, column, size):
    return value[row * size : (row + 1) * size, column * size : (column + 1) * size]


def forward_kernel(own, other, received, left, right, out):
    planes, length = received.shape[0], received.shape[1]
    stride = 2 * 2 * planes
    left, right = split(left[...]), split(right[...])
    for s, orbitals in enumerate((own, other)):
        for first in range(0, planes, BATCH):
            group = range(first, first + BATCH)
            fields = []
            for p in group:
                partner = received[p]
                fields.append(jnp.concatenate([orbitals[c, p] * partner for c in range(2)], axis=1))
            along_z = right_product(jnp.concatenate(fields, axis=0), right)
            blocks = [
                jnp.concatenate([tile(along_z, k, c, length) for k in range(BATCH)], axis=1)
                for c in range(2)
            ]
            both = left_product(left, jnp.concatenate(blocks, axis=0))
            for k, p in enumerate(group):
                for c in range(2):
                    row = (s * 2 + c) * planes + p
                    out[pl.ds(row, length, stride=stride), :] = tile(both, c, k, length)


def signed_wave(index, length):
    signed = jnp.where(index <= length // 2, index, index - length)
    return signed.astype(jnp.float32) * (2.0 * math.pi / length)


def middle_kernel(owner, occupied, field, forward, backward, out):
    sources, rows, fields, parts, lanes = field.shape
    planes = parts // 2
    length = sources * planes
    size = sources * parts
    ring = lax.axis_index("band") // RING
    weight = sum((occupied[j, owner[0]] == ring).astype(jnp.float32) for j in range(occupied.shape[0]))
    factor = weight * (-FRACTION * 4.0 * math.pi / float(length**3))
    row = lax.broadcasted_iota(jnp.int32, (size, lanes), 0)
    x_index = (row // parts) * planes + row % planes
    wave_x = signed_wave(x_index, length)
    wave_z = signed_wave(lax.broadcasted_iota(jnp.int32, (size, lanes), 1), length)
    flat = wave_x * wave_x + wave_z * wave_z + SCREEN
    forward, backward = split(forward[...]), split(backward[...])
    kernels = []
    for k in range(rows):
        wave_y = signed_wave(lax.axis_index("fft") * rows + k, length)
        kernels += [factor / (flat + wave_y * wave_y)] * fields
    items = [(k, s) for k in range(rows) for s in range(fields)]
    value = jnp.concatenate([field[:, k, s].reshape(size, lanes) for k, s in items], axis=1)
    value = left_product(forward, value) * jnp.concatenate(kernels, axis=1)
    value = left_product(backward, value)
    for n, (k, s) in enumerate(items):
        target = ring if s == 0 else 1 - ring
        part = value[:, n * lanes : (n + 1) * lanes]
        out[target, :, k] = part.reshape(sources, parts, lanes)


def backward_kernel(field, own, other, left, right, out, result, done):
    planes, length = own.shape[0], own.shape[1]
    ring = lax.axis_index("band") // RING
    partners = ((ring, own), (1 - ring, other))
    left, right = split(left[...]), split(right[...])
    copies = []
    for p in range(planes):
        blocks = []
        for c in range(2):
            rows = pl.ds(c * planes + p, length, stride=2 * planes)
            blocks.append(jnp.concatenate([field[j, rows, :] for j, _ in partners], axis=1))
        along_y = left_product(left, jnp.concatenate(blocks, axis=0))
        wide = [
            jnp.concatenate([tile(along_y, c, k, length) for c in range(2)], axis=1)
            for k in range(len(partners))
        ]
        both = right_product(jnp.concatenate(wide, axis=0), right)
        for c in range(2):
            result[c, p] = sum(
                tile(both, k, c, length) * partner[p] for k, (_, partner) in enumerate(partners)
            )
            copies.append(pltpu.make_async_copy(result.at[c, p], out.at[c, p], done.at[c, p]))
            copies[-1].start()
    for copy in copies:
        copy.wait()


def smem():
    return pl.BlockSpec(memory_space=pltpu.SMEM)


def vmem():
    return pl.BlockSpec(memory_space=pltpu.VMEM)


def call(kernel, shape, specs, flops, name, **options):
    options.setdefault("out_specs", vmem())
    return pl.pallas_call(
        kernel,
        out_shape=jax.ShapeDtypeStruct(shape, jnp.float32),
        in_specs=specs,
        compiler_params=pltpu.CompilerParams(vmem_limit_bytes=VMEM_LIMIT),
        cost_estimate=pl.CostEstimate(flops=flops, bytes_accessed=4 << 20, transcendentals=0),
        name=name,
        **options,
    )


def body(orbitals, owner, occupied):
    bands, planes, length, _ = orbitals.shape
    groups = lax.axis_size("band")
    columns = lax.axis_size("fft")
    rows = length // columns
    ring = RING
    order = occupied.T
    flops = 2 * 2 * 3 * 2 * (2 * length) * (2 * length) * planes * length

    swap = [(k, (k + ring) % groups) for k in range(groups)]
    with jax.named_scope("swap_orbitals"):
        other = lax.ppermute(orbitals, "band", swap)

    with jax.named_scope("scatter"):
        pieces = lax.all_to_all(orbitals.reshape(groups, -1, LANES), "band", 0, 0, tiled=True)
    mine = call(
        spread_kernel, (ring,) + pieces.shape[1:], [smem()] * 2 + [vmem()], 0, "spread"
    )(owner, order, pieces)
    rings = [[a * ring + y for y in range(ring)] for a in range(2)]
    with jax.named_scope("gather"):
        received = lax.all_to_all(mine, "band", 0, 0, axis_index_groups=rings, tiled=True)
    received = received.reshape(planes, length, length)

    matrix = wave_matrix(length)
    left, right = matrix, matrix.T.copy()
    x_index = np.arange(length).reshape(columns, 1, planes) + np.array([0, length])[None, :, None]
    x_index = x_index.reshape(-1)
    mixed = matrix[np.ix_(x_index, x_index)]
    x_forward, x_backward = mixed, mixed.T.copy()

    spectrum = call(
        forward_kernel, (length * 2 * 2 * planes, LANES), [vmem()] * 5, flops, "forward_zy"
    )(orbitals, other, received, left, right)
    with jax.named_scope("to_columns"):
        spectrum = lax.all_to_all(
            spectrum.reshape(columns, rows * 2 * 2 * planes, LANES), "fft", 0, 0, tiled=True
        )
    with jax.named_scope("swap_received"):
        received_other = lax.ppermute(received, "band", swap)
    spectrum = call(
        middle_kernel,
        (2, columns, rows, 2 * planes, LANES),
        [smem()] * 2 + [vmem()] * 3,
        flops,
        "solve_x",
    )(owner, order, spectrum.reshape(columns, rows, 2, 2 * planes, LANES), x_forward, x_backward)
    sharing = [
        [(a * ring + y) * columns + f for a in range(2) for f in range(columns)] for y in range(ring)
    ]
    with jax.named_scope("to_planes"):
        spectrum = lax.all_to_all(
            spectrum.reshape(2 * columns, rows * 2 * planes, LANES),
            ("band", "fft"),
            0,
            0,
            axis_index_groups=sharing,
            tiled=True,
        )
    return call(
        backward_kernel,
        orbitals.shape,
        [vmem()] * 5,
        flops,
        "backward_yz",
        out_specs=pl.BlockSpec(memory_space=pl.ANY),
        scratch_shapes=[
            pltpu.VMEM(orbitals.shape, jnp.float32),
            pltpu.SemaphoreType.DMA((bands, planes)),
        ],
    )(
        spectrum.reshape(2, columns * rows * 2 * planes, LANES),
        received,
        received_other,
        right,
        left,
    )


def solution(mesh):
    return jax.shard_map(
        body,
        mesh=mesh,
        in_specs=(P("band", "fft", None, None), P(), P()),
        out_specs=P("band", "fft", None, None),
        check_vma=False,
    )
```

```python
import math

import jax
import jax.numpy as jnp
import numpy as np
from jax import lax
from jax.experimental import pallas as pl
from jax.experimental.pallas import tpu as pltpu
from jax.sharding import PartitionSpec as P

SCREEN = 0.025
FRACTION = 0.25
LANES = 128
BATCH = 2
RING = 8
SHARES = 2
VMEM_LIMIT = 40 * 1024 * 1024


def wave_matrix(length):
    indices = np.arange(length)
    angles = (indices[:, None] * indices[None, :] % length) * (2.0 * math.pi / length)
    cosine, sine = np.cos(angles), np.sin(angles)
    return np.block([[cosine, sine], [-sine, cosine]]).astype(np.float32)


def split(value):
    high = value.astype(jnp.bfloat16)
    low = (value - high.astype(jnp.float32)).astype(jnp.bfloat16)
    return high, low


def dot(left, right):
    return jnp.dot(left, right, preferred_element_type=jnp.float32)


def left_product(matrix, value):
    high, low = split(value)
    return dot(matrix[0], high) + (dot(matrix[0], low) + dot(matrix[1], high))


def right_product(value, matrix):
    high, low = split(value)
    return dot(high, matrix[0]) + (dot(low, matrix[0]) + dot(high, matrix[1]))


def choice_kernel(owner, occupied, leader, weight):
    leader[...] = jnp.broadcast_to(owner[:, :1].astype(jnp.float32), leader.shape)
    ring = lax.axis_index("band") // RING
    group = lax.broadcasted_iota(jnp.int32, occupied.shape, 1)
    named = (group == owner[:, :1]) & (occupied[...] == ring)
    count = jnp.sum(jnp.where(named, 1.0, 0.0), axis=(0, 1), keepdims=True)
    weight[...] = jnp.broadcast_to(count, weight.shape)


def spread_kernel(leader, pieces, out):
    shape = pieces.shape[1:]
    chosen = jnp.broadcast_to(leader[:1], shape)
    piece = jnp.zeros(shape, jnp.float32)
    for k in range(pieces.shape[0]):
        piece = jnp.where(chosen == float(k), pieces[k], piece)
    for k in range(out.shape[0]):
        out[k] = piece


def tile(value, row, column, size):
    return value[row * size : (row + 1) * size, column * size : (column + 1) * size]


def forward_kernel(own, other, received, left, right, out):
    planes, length = received.shape[0], received.shape[1]
    stride = 2 * 2 * planes
    left, right = split(left[...]), split(right[...])
    for s, orbitals in enumerate((own, other)):
        for first in range(0, planes, BATCH):
            group = range(first, first + BATCH)
            fields = []
            for p in group:
                partner = received[p]
                fields.append(jnp.concatenate([orbitals[c, p] * partner for c in range(2)], axis=1))
            along_z = right_product(jnp.concatenate(fields, axis=0), right)
            blocks = [
                jnp.concatenate([tile(along_z, k, c, length) for k in range(BATCH)], axis=1)
                for c in range(2)
            ]
            both = left_product(left, jnp.concatenate(blocks, axis=0))
            for k, p in enumerate(group):
                for c in range(2):
                    row = (s * 2 + c) * planes + p
                    out[pl.ds(row, length, stride=stride), :] = tile(both, c, k, length)


def signed_wave(index, length):
    signed = jnp.where(index <= length // 2, index, index - length)
    return signed.astype(jnp.float32) * (2.0 * math.pi / length)


def middle_kernel(weight, field, forward, backward, out, result, done):
    sources, rows, fields, parts, lanes = field.shape
    planes = parts // 2
    length = sources * planes
    size = sources * parts
    ring = lax.axis_index("band") // RING
    factor = weight[:1] * (-FRACTION * 4.0 * math.pi / float(length**3))
    row = lax.broadcasted_iota(jnp.int32, (size, lanes), 0)
    x_index = (row // parts) * planes + row % planes
    wave_x = signed_wave(x_index, length)
    wave_z = signed_wave(lax.broadcasted_iota(jnp.int32, (size, lanes), 1), length)
    flat = wave_x * wave_x + wave_z * wave_z + SCREEN
    forward, backward = split(forward[...]), split(backward[...])
    kernels = []
    for k in range(rows):
        wave_y = signed_wave(lax.axis_index("fft") * rows + k, length)
        kernels += [factor / (flat + wave_y * wave_y)] * fields
    items = [(k, s) for k in range(rows) for s in range(fields)]
    value = jnp.concatenate([field[:, k, s].reshape(size, lanes) for k, s in items], axis=1)
    value = left_product(forward, value) * jnp.concatenate(kernels, axis=1)
    copies = []
    step = sources // SHARES
    for share in range(SHARES):
        part = slice(share * step, (share + 1) * step)
        matrix = [m[share * step * parts : (share + 1) * step * parts] for m in backward]
        solved = left_product(matrix, value)
        for n, (k, s) in enumerate(items):
            block = solved[:, n * lanes : (n + 1) * lanes]
            result[s, part, k] = block.reshape(step, parts, lanes)
        for s, target in enumerate((ring, 1 - ring)):
            copies.append(
                pltpu.make_async_copy(result.at[s, part], out.at[target, part], done.at[s, share])
            )
            copies[-1].start()
    for copy in copies:
        copy.wait()


def backward_kernel(field, own, other, left, right, out, result, done):
    planes, length = own.shape[0], own.shape[1]
    ring = lax.axis_index("band") // RING
    partners = ((ring, own), (1 - ring, other))
    left, right = split(left[...]), split(right[...])
    copies = []
    for p in range(planes):
        blocks = []
        for c in range(2):
            rows = pl.ds(c * planes + p, length, stride=2 * planes)
            blocks.append(jnp.concatenate([field[j, rows, :] for j, _ in partners], axis=1))
        along_y = left_product(left, jnp.concatenate(blocks, axis=0))
        wide = [
            jnp.concatenate([tile(along_y, c, k, length) for c in range(2)], axis=1)
            for k in range(len(partners))
        ]
        both = right_product(jnp.concatenate(wide, axis=0), right)
        for c in range(2):
            result[c, p] = sum(
                tile(both, k, c, length) * partner[p] for k, (_, partner) in enumerate(partners)
            )
            copies.append(pltpu.make_async_copy(result.at[c, p], out.at[c, p], done.at[c, p]))
            copies[-1].start()
    for copy in copies:
        copy.wait()


def vmem():
    return pl.BlockSpec(memory_space=pltpu.VMEM)


def is_shape(value):
    return isinstance(value, tuple)


def call(kernel, shape, specs, flops, name, **options):
    options.setdefault("out_specs", vmem())
    return pl.pallas_call(
        kernel,
        out_shape=jax.tree.map(lambda s: jax.ShapeDtypeStruct(s, jnp.float32), shape, is_leaf=is_shape),
        in_specs=specs,
        compiler_params=pltpu.CompilerParams(vmem_limit_bytes=VMEM_LIMIT),
        cost_estimate=pl.CostEstimate(flops=flops, bytes_accessed=4 << 20, transcendentals=0),
        name=name,
        **options,
    )


def body(orbitals, owner, occupied):
    bands, planes, length, _ = orbitals.shape
    groups = lax.axis_size("band")
    columns = lax.axis_size("fft")
    rows = length // columns
    ring = RING
    order = occupied.T
    flops = 2 * 2 * 3 * 2 * (2 * length) * (2 * length) * planes * length

    swap = [(k, (k + ring) % groups) for k in range(groups)]
    with jax.named_scope("swap_orbitals"):
        other = lax.ppermute(orbitals, "band", swap)

    with jax.named_scope("scatter"):
        pieces = lax.all_to_all(orbitals.reshape(groups, -1, LANES), "band", 0, 0, tiled=True)
    leader, weight = call(
        choice_kernel,
        [(8, LANES)] * 2,
        [vmem()] * 2,
        flops // 2,
        "choice",
        out_specs=[vmem()] * 2,
    )(owner.reshape(1, -1), order)
    mine = call(spread_kernel, (ring,) + pieces.shape[1:], [vmem()] * 2, 0, "spread")(leader, pieces)
    rings = [[a * ring + y for y in range(ring)] for a in range(2)]
    with jax.named_scope("gather"):
        received = lax.all_to_all(mine, "band", 0, 0, axis_index_groups=rings, tiled=True)
    received = received.reshape(planes, length, length)

    matrix = wave_matrix(length)
    left, right = matrix, matrix.T.copy()
    x_index = np.arange(length).reshape(columns, 1, planes) + np.array([0, length])[None, :, None]
    x_index = x_index.reshape(-1)
    mixed = matrix[np.ix_(x_index, x_index)]
    x_forward, x_backward = mixed, mixed.T.copy()

    spectrum = call(
        forward_kernel, (length * 2 * 2 * planes, LANES), [vmem()] * 5, flops, "forward_zy"
    )(orbitals, other, received, left, right)
    with jax.named_scope("to_columns"):
        spectrum = lax.all_to_all(
            spectrum.reshape(columns, rows * 2 * 2 * planes, LANES), "fft", 0, 0, tiled=True
        )
    with jax.named_scope("swap_received"):
        received_other = lax.ppermute(received, "band", swap)
    spectrum = call(
        middle_kernel,
        (2, columns, rows, 2 * planes, LANES),
        [vmem()] * 4,
        flops,
        "solve_x",
        out_specs=pl.BlockSpec(memory_space=pl.ANY),
        scratch_shapes=[
            pltpu.VMEM((2, columns, rows, 2 * planes, LANES), jnp.float32),
            pltpu.SemaphoreType.DMA((2, SHARES)),
        ],
    )(weight, spectrum.reshape(columns, rows, 2, 2 * planes, LANES), x_forward, x_backward)
    sharing = [
        [(a * ring + y) * columns + f for a in range(2) for f in range(columns)] for y in range(ring)
    ]
    with jax.named_scope("to_planes"):
        spectrum = lax.all_to_all(
            spectrum.reshape(2 * columns, rows * 2 * planes, LANES),
            ("band", "fft"),
            0,
            0,
            axis_index_groups=sharing,
            tiled=True,
        )
    return call(
        backward_kernel,
        orbitals.shape,
        [vmem()] * 5,
        flops,
        "backward_yz",
        out_specs=pl.BlockSpec(memory_space=pl.ANY),
        scratch_shapes=[
            pltpu.VMEM(orbitals.shape, jnp.float32),
            pltpu.SemaphoreType.DMA((bands, planes)),
        ],
    )(
        spectrum.reshape(2, columns * rows * 2 * planes, LANES),
        received,
        received_other,
        right,
        left,
    )


def solution(mesh):
    return jax.shard_map(
        body,
        mesh=mesh,
        in_specs=(P("band", "fft", None, None), P(), P()),
        out_specs=P("band", "fft", None, None),
        check_vma=False,
    )
```

```python
import math

import jax
import jax.numpy as jnp
import numpy as np
from jax import lax
from jax.experimental import pallas as pl
from jax.experimental.pallas import tpu as pltpu
from jax.sharding import PartitionSpec as P

SCREEN = 0.025
FRACTION = 0.25
LANES = 128
BATCH = 2
RING = 8
SHARES = 2
PLANES = 4
VMEM_LIMIT = 40 * 1024 * 1024


def wave_matrix(length):
    indices = np.arange(length)
    angles = (indices[:, None] * indices[None, :] % length) * (2.0 * math.pi / length)
    cosine, sine = np.cos(angles), np.sin(angles)
    return np.block([[cosine, sine], [-sine, cosine]]).astype(np.float32)


def split(value):
    high = value.astype(jnp.bfloat16)
    low = (value - high.astype(jnp.float32)).astype(jnp.bfloat16)
    return high, low


def dot(left, right):
    return jnp.dot(left, right, preferred_element_type=jnp.float32)


def left_product(matrix, value):
    high, low = split(value)
    return dot(matrix[0], high) + (dot(matrix[0], low) + dot(matrix[1], high))


def right_product(value, matrix):
    high, low = split(value)
    return dot(high, matrix[0]) + (dot(low, matrix[0]) + dot(high, matrix[1]))


def choice_kernel(owner, occupied, leader, weight):
    leader[...] = jnp.broadcast_to(owner[:, :1].astype(jnp.float32), leader.shape)
    ring = lax.axis_index("band") // RING
    group = lax.broadcasted_iota(jnp.int32, occupied.shape, 1)
    named = (group == owner[:, :1]) & (occupied[...] == ring)
    count = jnp.sum(jnp.where(named, 1.0, 0.0), axis=(0, 1), keepdims=True)
    weight[...] = jnp.broadcast_to(count, weight.shape)


def spread_kernel(leader, pieces, out):
    shape = pieces.shape[1:]
    chosen = jnp.broadcast_to(leader[:1], shape)
    piece = jnp.zeros(shape, jnp.float32)
    for k in range(pieces.shape[0]):
        piece = jnp.where(chosen == float(k), pieces[k], piece)
    for k in range(out.shape[0]):
        out[k] = piece


def tile(value, row, column, size):
    return value[row * size : (row + 1) * size, column * size : (column + 1) * size]


def forward_kernel(own, other, received, left, right, out):
    planes, length = received.shape[0], received.shape[1]
    stride = 2 * 2 * planes
    left, right = split(left[...]), split(right[...])
    for s, orbitals in enumerate((own, other)):
        for first in range(0, planes, BATCH):
            group = range(first, first + BATCH)
            fields = []
            for p in group:
                partner = received[p]
                fields.append(jnp.concatenate([orbitals[c, p] * partner for c in range(2)], axis=1))
            along_z = right_product(jnp.concatenate(fields, axis=0), right)
            blocks = [
                jnp.concatenate([tile(along_z, k, c, length) for k in range(BATCH)], axis=1)
                for c in range(2)
            ]
            both = left_product(left, jnp.concatenate(blocks, axis=0))
            for k, p in enumerate(group):
                for c in range(2):
                    row = (s * 2 + c) * planes + p
                    out[pl.ds(row, length, stride=stride), :] = tile(both, c, k, length)


def signed_wave(index, length):
    signed = jnp.where(index <= length // 2, index, index - length)
    return signed.astype(jnp.float32) * (2.0 * math.pi / length)


def middle_kernel(weight, field, forward, backward, out, result, done):
    sources, rows, fields, parts, lanes = field.shape
    planes = parts // 2
    length = sources * planes
    size = sources * parts
    ring = lax.axis_index("band") // RING
    factor = weight[:1] * (-FRACTION * 4.0 * math.pi / float(length**3))
    row = lax.broadcasted_iota(jnp.int32, (size, lanes), 0)
    x_index = (row // parts) * planes + row % planes
    wave_x = signed_wave(x_index, length)
    wave_z = signed_wave(lax.broadcasted_iota(jnp.int32, (size, lanes), 1), length)
    flat = wave_x * wave_x + wave_z * wave_z + SCREEN
    forward, backward = split(forward[...]), split(backward[...])
    kernels = []
    for k in range(rows):
        wave_y = signed_wave(lax.axis_index("fft") * rows + k, length)
        kernels += [factor / (flat + wave_y * wave_y)] * fields
    items = [(k, s) for k in range(rows) for s in range(fields)]
    value = jnp.concatenate([field[:, k, s].reshape(size, lanes) for k, s in items], axis=1)
    value = left_product(forward, value) * jnp.concatenate(kernels, axis=1)
    copies = []
    step = sources // SHARES
    for share in range(SHARES):
        part = slice(share * step, (share + 1) * step)
        matrix = [m[share * step * parts : (share + 1) * step * parts] for m in backward]
        solved = left_product(matrix, value)
        for n, (k, s) in enumerate(items):
            block = solved[:, n * lanes : (n + 1) * lanes]
            result[s, part, k] = block.reshape(step, parts, lanes)
        for s, target in enumerate((ring, 1 - ring)):
            copies.append(
                pltpu.make_async_copy(result.at[s, part], out.at[target, part], done.at[s, share])
            )
            copies[-1].start()
    for copy in copies:
        copy.wait()


def backward_kernel(field, own, other, left, right, out, result, done):
    planes, length = own.shape[0], own.shape[1]
    ring = lax.axis_index("band") // RING
    partners = ((ring, own), (1 - ring, other))
    left, right = split(left[...]), split(right[...])
    copies = []
    for first in range(0, planes, PLANES):
        group = range(first, first + PLANES)
        blocks = []
        for c in range(2):
            rows = [pl.ds(c * planes + p, length, stride=2 * planes) for p in group]
            blocks.append(
                jnp.concatenate([field[j, row, :] for row in rows for j, _ in partners], axis=1)
            )
        along_y = left_product(left, jnp.concatenate(blocks, axis=0))
        wide = [
            jnp.concatenate([tile(along_y, c, k, length) for c in range(2)], axis=1)
            for k in range(PLANES * len(partners))
        ]
        both = right_product(jnp.concatenate(wide, axis=0), right)
        for n, p in enumerate(group):
            for c in range(2):
                result[c, p] = sum(
                    tile(both, n * len(partners) + k, c, length) * partner[p]
                    for k, (_, partner) in enumerate(partners)
                )
                copies.append(pltpu.make_async_copy(result.at[c, p], out.at[c, p], done.at[c, p]))
                copies[-1].start()
    for copy in copies:
        copy.wait()


def vmem():
    return pl.BlockSpec(memory_space=pltpu.VMEM)


def is_shape(value):
    return isinstance(value, tuple)


def call(kernel, shape, specs, flops, name, **options):
    options.setdefault("out_specs", vmem())
    return pl.pallas_call(
        kernel,
        out_shape=jax.tree.map(lambda s: jax.ShapeDtypeStruct(s, jnp.float32), shape, is_leaf=is_shape),
        in_specs=specs,
        compiler_params=pltpu.CompilerParams(vmem_limit_bytes=VMEM_LIMIT),
        cost_estimate=pl.CostEstimate(flops=flops, bytes_accessed=4 << 20, transcendentals=0),
        name=name,
        **options,
    )


def body(orbitals, owner, occupied):
    bands, planes, length, _ = orbitals.shape
    groups = lax.axis_size("band")
    columns = lax.axis_size("fft")
    rows = length // columns
    ring = RING
    order = occupied.T
    flops = 2 * 2 * 3 * 2 * (2 * length) * (2 * length) * planes * length

    swap = [(k, (k + ring) % groups) for k in range(groups)]
    with jax.named_scope("swap_orbitals"):
        other = lax.ppermute(orbitals, "band", swap)

    with jax.named_scope("scatter"):
        pieces = lax.all_to_all(orbitals.reshape(groups, -1, LANES), "band", 0, 0, tiled=True)
    leader, weight = call(
        choice_kernel,
        [(8, LANES)] * 2,
        [vmem()] * 2,
        flops // 2,
        "choice",
        out_specs=[vmem()] * 2,
    )(owner.reshape(1, -1), order)
    mine = call(spread_kernel, (ring,) + pieces.shape[1:], [vmem()] * 2, 0, "spread")(leader, pieces)
    rings = [[a * ring + y for y in range(ring)] for a in range(2)]
    with jax.named_scope("gather"):
        received = lax.all_to_all(mine, "band", 0, 0, axis_index_groups=rings, tiled=True)
    received = received.reshape(planes, length, length)

    matrix = wave_matrix(length)
    left, right = matrix, matrix.T.copy()
    x_index = np.arange(length).reshape(columns, 1, planes) + np.array([0, length])[None, :, None]
    x_index = x_index.reshape(-1)
    mixed = matrix[np.ix_(x_index, x_index)]
    x_forward, x_backward = mixed, mixed.T.copy()

    spectrum = call(
        forward_kernel, (length * 2 * 2 * planes, LANES), [vmem()] * 5, flops, "forward_zy"
    )(orbitals, other, received, left, right)
    with jax.named_scope("to_columns"):
        spectrum = lax.all_to_all(
            spectrum.reshape(columns, rows * 2 * 2 * planes, LANES), "fft", 0, 0, tiled=True
        )
    with jax.named_scope("swap_received"):
        received_other = lax.ppermute(received, "band", swap)
    spectrum = call(
        middle_kernel,
        (2, columns, rows, 2 * planes, LANES),
        [vmem()] * 4,
        flops,
        "solve_x",
        out_specs=pl.BlockSpec(memory_space=pl.ANY),
        scratch_shapes=[
            pltpu.VMEM((2, columns, rows, 2 * planes, LANES), jnp.float32),
            pltpu.SemaphoreType.DMA((2, SHARES)),
        ],
    )(weight, spectrum.reshape(columns, rows, 2, 2 * planes, LANES), x_forward, x_backward)
    sharing = [
        [(a * ring + y) * columns + f for a in range(2) for f in range(columns)] for y in range(ring)
    ]
    with jax.named_scope("to_planes"):
        spectrum = lax.all_to_all(
            spectrum.reshape(2 * columns, rows * 2 * planes, LANES),
            ("band", "fft"),
            0,
            0,
            axis_index_groups=sharing,
            tiled=True,
        )
    return call(
        backward_kernel,
        orbitals.shape,
        [vmem()] * 5,
        flops,
        "backward_yz",
        out_specs=pl.BlockSpec(memory_space=pl.ANY),
        scratch_shapes=[
            pltpu.VMEM(orbitals.shape, jnp.float32),
            pltpu.SemaphoreType.DMA((bands, planes)),
        ],
    )(
        spectrum.reshape(2, columns * rows * 2 * planes, LANES),
        received,
        received_other,
        right,
        left,
    )


def solution(mesh):
    return jax.shard_map(
        body,
        mesh=mesh,
        in_specs=(P("band", "fft", None, None), P(), P()),
        out_specs=P("band", "fft", None, None),
        check_vma=False,
    )
```

```python
import math

import jax
import jax.numpy as jnp
import numpy as np
from jax import lax
from jax.experimental import pallas as pl
from jax.experimental.pallas import tpu as pltpu
from jax.sharding import PartitionSpec as P

SCREEN = 0.025
FRACTION = 0.25
LANES = 128
BATCH = 2
RING = 8
PLACES = (0, 4, 2, 6, 1, 5, 3, 7)
SHARES = 2
PLANES = 4
VMEM_LIMIT = 40 * 1024 * 1024


def wave_matrix(length):
    indices = np.arange(length)
    angles = (indices[:, None] * indices[None, :] % length) * (2.0 * math.pi / length)
    cosine, sine = np.cos(angles), np.sin(angles)
    return np.block([[cosine, sine], [-sine, cosine]]).astype(np.float32)


def split(value):
    high = value.astype(jnp.bfloat16)
    low = (value - high.astype(jnp.float32)).astype(jnp.bfloat16)
    return high, low


def dot(left, right):
    return jnp.dot(left, right, preferred_element_type=jnp.float32)


def left_product(matrix, value):
    high, low = split(value)
    return dot(matrix[0], high) + (dot(matrix[0], low) + dot(matrix[1], high))


def right_product(value, matrix):
    high, low = split(value)
    return dot(high, matrix[0]) + (dot(low, matrix[0]) + dot(high, matrix[1]))


def choice_kernel(owner, occupied, leader, weight):
    leader[...] = jnp.broadcast_to(owner[:, :1].astype(jnp.float32), leader.shape)
    ring = lax.axis_index("band") // RING
    group = lax.broadcasted_iota(jnp.int32, occupied.shape, 1)
    named = (group == owner[:, :1]) & (occupied[...] == ring)
    count = jnp.sum(jnp.where(named, 1.0, 0.0), axis=(0, 1), keepdims=True)
    weight[...] = jnp.broadcast_to(count, weight.shape)


def spread_kernel(leader, pieces, out):
    shape = pieces.shape[1:]
    chosen = jnp.broadcast_to(leader[:1], shape)
    piece = jnp.zeros(shape, jnp.float32)
    for k in range(pieces.shape[0]):
        piece = jnp.where(chosen == float(k), pieces[k], piece)
    for k in range(out.shape[0]):
        out[k] = piece


def tile(value, row, column, size):
    return value[row * size : (row + 1) * size, column * size : (column + 1) * size]


def plane(received, p):
    pieces = len(PLACES) // (received.shape[0] * received.shape[1] // LANES)
    return jnp.concatenate(
        [received[PLACES.index(p * pieces + k)] for k in range(pieces)], axis=0
    )


def forward_kernel(own, other, received, left, right, out):
    planes, length = own.shape[1], own.shape[2]
    stride = 2 * 2 * planes
    left, right = split(left[...]), split(right[...])
    for s, orbitals in enumerate((own, other)):
        for first in range(0, planes, BATCH):
            group = range(first, first + BATCH)
            fields = []
            for p in group:
                partner = plane(received, p)
                fields.append(jnp.concatenate([orbitals[c, p] * partner for c in range(2)], axis=1))
            along_z = right_product(jnp.concatenate(fields, axis=0), right)
            blocks = [
                jnp.concatenate([tile(along_z, k, c, length) for k in range(BATCH)], axis=1)
                for c in range(2)
            ]
            both = left_product(left, jnp.concatenate(blocks, axis=0))
            for k, p in enumerate(group):
                for c in range(2):
                    row = (s * 2 + c) * planes + p
                    out[pl.ds(row, length, stride=stride), :] = tile(both, c, k, length)


def signed_wave(index, length):
    signed = jnp.where(index <= length // 2, index, index - length)
    return signed.astype(jnp.float32) * (2.0 * math.pi / length)


def middle_kernel(weight, field, forward, backward, out, result, done):
    sources, rows, fields, parts, lanes = field.shape
    planes = parts // 2
    length = sources * planes
    size = sources * parts
    ring = lax.axis_index("band") // RING
    factor = weight[:1] * (-FRACTION * 4.0 * math.pi / float(length**3))
    row = lax.broadcasted_iota(jnp.int32, (size, lanes), 0)
    x_index = (row // parts) * planes + row % planes
    wave_x = signed_wave(x_index, length)
    wave_z = signed_wave(lax.broadcasted_iota(jnp.int32, (size, lanes), 1), length)
    flat = wave_x * wave_x + wave_z * wave_z + SCREEN
    forward, backward = split(forward[...]), split(backward[...])
    kernels = []
    for k in range(rows):
        wave_y = signed_wave(lax.axis_index("fft") * rows + k, length)
        kernels += [factor / (flat + wave_y * wave_y)] * fields
    items = [(k, s) for k in range(rows) for s in range(fields)]
    value = jnp.concatenate([field[:, k, s].reshape(size, lanes) for k, s in items], axis=1)
    value = left_product(forward, value) * jnp.concatenate(kernels, axis=1)
    copies = []
    step = sources // SHARES
    for share in range(SHARES):
        part = slice(share * step, (share + 1) * step)
        matrix = [m[share * step * parts : (share + 1) * step * parts] for m in backward]
        solved = left_product(matrix, value)
        for n, (k, s) in enumerate(items):
            block = solved[:, n * lanes : (n + 1) * lanes]
            result[s, part, k] = block.reshape(step, parts, lanes)
        for s, target in enumerate((ring, 1 - ring)):
            copies.append(
                pltpu.make_async_copy(result.at[s, part], out.at[target, part], done.at[s, share])
            )
            copies[-1].start()
    for copy in copies:
        copy.wait()


def backward_kernel(field, own, other, left, right, out, result, done):
    planes, length = result.shape[1], result.shape[2]
    ring = lax.axis_index("band") // RING
    partners = ((ring, own), (1 - ring, other))
    left, right = split(left[...]), split(right[...])
    copies = []
    for first in range(0, planes, PLANES):
        group = range(first, first + PLANES)
        blocks = []
        for c in range(2):
            rows = [pl.ds(c * planes + p, length, stride=2 * planes) for p in group]
            blocks.append(
                jnp.concatenate([field[j, row, :] for row in rows for j, _ in partners], axis=1)
            )
        along_y = left_product(left, jnp.concatenate(blocks, axis=0))
        wide = [
            jnp.concatenate([tile(along_y, c, k, length) for c in range(2)], axis=1)
            for k in range(PLANES * len(partners))
        ]
        both = right_product(jnp.concatenate(wide, axis=0), right)
        for n, p in enumerate(group):
            for c in range(2):
                result[c, p] = sum(
                    tile(both, n * len(partners) + k, c, length) * plane(partner, p)
                    for k, (_, partner) in enumerate(partners)
                )
                copies.append(pltpu.make_async_copy(result.at[c, p], out.at[c, p], done.at[c, p]))
                copies[-1].start()
    for copy in copies:
        copy.wait()


def vmem():
    return pl.BlockSpec(memory_space=pltpu.VMEM)


def is_shape(value):
    return isinstance(value, tuple)


def call(kernel, shape, specs, flops, name, **options):
    options.setdefault("out_specs", vmem())
    return pl.pallas_call(
        kernel,
        out_shape=jax.tree.map(lambda s: jax.ShapeDtypeStruct(s, jnp.float32), shape, is_leaf=is_shape),
        in_specs=specs,
        compiler_params=pltpu.CompilerParams(vmem_limit_bytes=VMEM_LIMIT),
        cost_estimate=pl.CostEstimate(flops=flops, bytes_accessed=4 << 20, transcendentals=0),
        name=name,
        **options,
    )


def body(orbitals, owner, occupied):
    bands, planes, length, _ = orbitals.shape
    groups = lax.axis_size("band")
    columns = lax.axis_size("fft")
    rows = length // columns
    ring = RING
    order = occupied.T
    flops = 2 * 2 * 3 * 2 * (2 * length) * (2 * length) * planes * length

    swap = [(k, (k + ring) % groups) for k in range(groups)]
    with jax.named_scope("swap_orbitals"):
        other = lax.ppermute(orbitals, "band", swap)

    with jax.named_scope("scatter"):
        pieces = lax.all_to_all(orbitals.reshape(groups, -1, LANES), "band", 0, 0, tiled=True)
    leader, weight = call(
        choice_kernel,
        [(8, LANES)] * 2,
        [vmem()] * 2,
        flops // 2,
        "choice",
        out_specs=[vmem()] * 2,
    )(owner.reshape(1, -1), order)
    mine = call(spread_kernel, (ring,) + pieces.shape[1:], [vmem()] * 2, 0, "spread")(leader, pieces)
    rings = [[a * ring + y for y in PLACES] for a in range(2)]
    with jax.named_scope("gather"):
        received = lax.all_to_all(mine, "band", 0, 0, axis_index_groups=rings, tiled=True)

    matrix = wave_matrix(length)
    left, right = matrix, matrix.T.copy()
    x_index = np.arange(length).reshape(columns, 1, planes) + np.array([0, length])[None, :, None]
    x_index = x_index.reshape(-1)
    mixed = matrix[np.ix_(x_index, x_index)]
    x_forward, x_backward = mixed, mixed.T.copy()

    spectrum = call(
        forward_kernel, (length * 2 * 2 * planes, LANES), [vmem()] * 5, flops, "forward_zy"
    )(orbitals, other, received, left, right)
    with jax.named_scope("to_columns"):
        spectrum = lax.all_to_all(
            spectrum.reshape(columns, rows * 2 * 2 * planes, LANES), "fft", 0, 0, tiled=True
        )
    with jax.named_scope("swap_received"):
        received_other = lax.ppermute(received, "band", swap)
    spectrum = call(
        middle_kernel,
        (2, columns, rows, 2 * planes, LANES),
        [vmem()] * 4,
        flops,
        "solve_x",
        out_specs=pl.BlockSpec(memory_space=pl.ANY),
        scratch_shapes=[
            pltpu.VMEM((2, columns, rows, 2 * planes, LANES), jnp.float32),
            pltpu.SemaphoreType.DMA((2, SHARES)),
        ],
    )(weight, spectrum.reshape(columns, rows, 2, 2 * planes, LANES), x_forward, x_backward)
    sharing = [
        [(a * ring + y) * columns + f for a in range(2) for f in range(columns)] for y in range(ring)
    ]
    with jax.named_scope("to_planes"):
        spectrum = lax.all_to_all(
            spectrum.reshape(2 * columns, rows * 2 * planes, LANES),
            ("band", "fft"),
            0,
            0,
            axis_index_groups=sharing,
            tiled=True,
        )
    return call(
        backward_kernel,
        orbitals.shape,
        [vmem()] * 5,
        flops,
        "backward_yz",
        out_specs=pl.BlockSpec(memory_space=pl.ANY),
        scratch_shapes=[
            pltpu.VMEM(orbitals.shape, jnp.float32),
            pltpu.SemaphoreType.DMA((bands, planes)),
        ],
    )(
        spectrum.reshape(2, columns * rows * 2 * planes, LANES),
        received,
        received_other,
        right,
        left,
    )


def solution(mesh):
    return jax.shard_map(
        body,
        mesh=mesh,
        in_specs=(P("band", "fft", None, None), P(), P()),
        out_specs=P("band", "fft", None, None),
        check_vma=False,
    )
```

```python
import math

import jax
import jax.numpy as jnp
import numpy as np
from jax import lax
from jax.experimental import pallas as pl
from jax.experimental.pallas import tpu as pltpu
from jax.sharding import PartitionSpec as P

SCREEN = 0.025
FRACTION = 0.25
LANES = 128
BATCH = 2
RING = 8
PLACES = (0, 4, 2, 6, 1, 5, 3, 7)
SHARES = 2
PLANES = 4
MATRICES = 4
VMEM_LIMIT = 40 * 1024 * 1024


def wave_matrix(length):
    indices = np.arange(length)
    angles = (indices[:, None] * indices[None, :] % length) * (2.0 * math.pi / length)
    cosine, sine = np.cos(angles), np.sin(angles)
    return np.block([[cosine, sine], [-sine, cosine]]).astype(np.float32)


def split(value):
    high = value.astype(jnp.bfloat16)
    low = (value - high.astype(jnp.float32)).astype(jnp.bfloat16)
    return high, low


def dot(left, right):
    return jnp.dot(left, right, preferred_element_type=jnp.float32)


def left_product(matrix, value):
    high, low = split(value)
    return dot(matrix[0], high) + (dot(matrix[0], low) + dot(matrix[1], high))


def right_product(value, matrix):
    high, low = split(value)
    return dot(high, matrix[0]) + (dot(low, matrix[0]) + dot(high, matrix[1]))


def prepare_kernel(owner, occupied, *refs):
    matrices, (leader, *parts, table) = refs[:MATRICES], refs[MATRICES:]
    leader[...] = jnp.broadcast_to(owner[:, :1].astype(jnp.float32), leader.shape)
    for matrix, part in zip(matrices, parts):
        part[0], part[1] = split(matrix[...])
    ring = lax.axis_index("band") // RING
    group = lax.broadcasted_iota(jnp.int32, occupied.shape, 1)
    named = (group == owner[:, :1]) & (occupied[...] == ring)
    count = jnp.sum(jnp.where(named, 1.0, 0.0), axis=(0, 1), keepdims=True)
    rows, size, lanes = table.shape
    length = size // 2
    planes = length // lax.axis_size("fft")
    row = lax.broadcasted_iota(jnp.int32, (size, lanes), 0)
    wave_x = signed_wave((row // (2 * planes)) * planes + row % planes, length)
    wave_z = signed_wave(lax.broadcasted_iota(jnp.int32, (size, lanes), 1), length)
    flat = wave_x * wave_x + wave_z * wave_z + SCREEN
    factor = count * (-FRACTION * 4.0 * math.pi / float(length**3))
    for k in range(rows):
        wave_y = signed_wave(lax.axis_index("fft") * rows + k, length)
        table[k] = factor / (flat + wave_y * wave_y)


def spread_kernel(leader, pieces, out):
    shape = pieces.shape[1:]
    chosen = jnp.broadcast_to(leader[:1], shape)
    piece = jnp.zeros(shape, jnp.float32)
    for k in range(pieces.shape[0]):
        piece = jnp.where(chosen == float(k), pieces[k], piece)
    for k in range(out.shape[0]):
        out[k] = piece


def tile(value, row, column, size):
    return value[row * size : (row + 1) * size, column * size : (column + 1) * size]


def plane(received, p):
    pieces = len(PLACES) // (received.shape[0] * received.shape[1] // LANES)
    return jnp.concatenate(
        [received[PLACES.index(p * pieces + k)] for k in range(pieces)], axis=0
    )


def forward_kernel(own, other, received, left, right, out):
    planes, length = own.shape[1], own.shape[2]
    stride = 2 * 2 * planes
    for s, orbitals in enumerate((own, other)):
        for first in range(0, planes, BATCH):
            group = range(first, first + BATCH)
            fields = []
            for p in group:
                partner = plane(received, p)
                fields.append(jnp.concatenate([orbitals[c, p] * partner for c in range(2)], axis=1))
            along_z = right_product(jnp.concatenate(fields, axis=0), right)
            blocks = [
                jnp.concatenate([tile(along_z, k, c, length) for k in range(BATCH)], axis=1)
                for c in range(2)
            ]
            both = left_product(left, jnp.concatenate(blocks, axis=0))
            for k, p in enumerate(group):
                for c in range(2):
                    row = (s * 2 + c) * planes + p
                    out[pl.ds(row, length, stride=stride), :] = tile(both, c, k, length)


def signed_wave(index, length):
    signed = jnp.where(index <= length // 2, index, index - length)
    return signed.astype(jnp.float32) * (2.0 * math.pi / length)


def middle_kernel(table, field, forward, backward, out, result, done):
    sources, rows, fields, parts, lanes = field.shape
    size = sources * parts
    ring = lax.axis_index("band") // RING
    items = [(k, s) for k in range(rows) for s in range(fields)]
    value = jnp.concatenate([field[:, k, s].reshape(size, lanes) for k, s in items], axis=1)
    kernels = jnp.concatenate([table[k] for k, _ in items], axis=1)
    value = left_product(forward, value) * kernels
    copies = []
    step = sources // SHARES
    for share in range(SHARES):
        part = slice(share * step, (share + 1) * step)
        matrix = [backward[h, share * step * parts : (share + 1) * step * parts] for h in range(2)]
        solved = left_product(matrix, value)
        for n, (k, s) in enumerate(items):
            block = solved[:, n * lanes : (n + 1) * lanes]
            result[s, part, k] = block.reshape(step, parts, lanes)
        for s, target in enumerate((ring, 1 - ring)):
            copies.append(
                pltpu.make_async_copy(result.at[s, part], out.at[target, part], done.at[s, share])
            )
            copies[-1].start()
    for copy in copies:
        copy.wait()


def backward_kernel(field, own, other, left, right, out, result, done):
    planes, length = result.shape[1], result.shape[2]
    ring = lax.axis_index("band") // RING
    partners = ((ring, own), (1 - ring, other))
    copies = []
    for first in range(0, planes, PLANES):
        group = range(first, first + PLANES)
        blocks = []
        for c in range(2):
            rows = [pl.ds(c * planes + p, length, stride=2 * planes) for p in group]
            blocks.append(
                jnp.concatenate([field[j, row, :] for row in rows for j, _ in partners], axis=1)
            )
        along_y = left_product(left, jnp.concatenate(blocks, axis=0))
        wide = [
            jnp.concatenate([tile(along_y, c, k, length) for c in range(2)], axis=1)
            for k in range(PLANES * len(partners))
        ]
        both = right_product(jnp.concatenate(wide, axis=0), right)
        for n, p in enumerate(group):
            for c in range(2):
                result[c, p] = sum(
                    tile(both, n * len(partners) + k, c, length) * plane(partner, p)
                    for k, (_, partner) in enumerate(partners)
                )
                copies.append(pltpu.make_async_copy(result.at[c, p], out.at[c, p], done.at[c, p]))
                copies[-1].start()
    for copy in copies:
        copy.wait()


def vmem():
    return pl.BlockSpec(memory_space=pltpu.VMEM)


def call(kernel, shape, specs, flops, name, types=jnp.float32, **options):
    options.setdefault("out_specs", vmem())
    if isinstance(shape, list):
        out_shape = [jax.ShapeDtypeStruct(s, t) for s, t in zip(shape, types)]
    else:
        out_shape = jax.ShapeDtypeStruct(shape, types)
    return pl.pallas_call(
        kernel,
        out_shape=out_shape,
        in_specs=specs,
        compiler_params=pltpu.CompilerParams(vmem_limit_bytes=VMEM_LIMIT),
        cost_estimate=pl.CostEstimate(flops=flops, bytes_accessed=4 << 20, transcendentals=0),
        name=name,
        **options,
    )


def body(orbitals, owner, occupied):
    bands, planes, length, _ = orbitals.shape
    groups = lax.axis_size("band")
    columns = lax.axis_size("fft")
    rows = length // columns
    ring = RING
    order = occupied.T
    flops = 2 * 2 * 3 * 2 * (2 * length) * (2 * length) * planes * length

    swap = [(k, (k + ring) % groups) for k in range(groups)]
    with jax.named_scope("swap_orbitals"):
        other = lax.ppermute(orbitals, "band", swap)

    with jax.named_scope("scatter"):
        pieces = lax.all_to_all(orbitals.reshape(groups, -1, LANES), "band", 0, 0, tiled=True)
    matrix = wave_matrix(length)
    x_index = np.arange(length).reshape(columns, 1, planes) + np.array([0, length])[None, :, None]
    x_index = x_index.reshape(-1)
    mixed = matrix[np.ix_(x_index, x_index)]
    leader, left, right, x_forward, x_backward, table = call(
        prepare_kernel,
        [(8, LANES)] + [(2, 2 * length, 2 * length)] * MATRICES + [(rows, 2 * length, LANES)],
        [vmem()] * (2 + MATRICES),
        flops,
        "prepare",
        types=[jnp.float32] + [jnp.bfloat16] * MATRICES + [jnp.float32],
        out_specs=[vmem()] * (2 + MATRICES),
    )(owner.reshape(1, -1), order, matrix, matrix.T.copy(), mixed, mixed.T.copy())
    mine = call(spread_kernel, (ring,) + pieces.shape[1:], [vmem()] * 2, 0, "spread")(leader, pieces)
    rings = [[a * ring + y for y in PLACES] for a in range(2)]
    with jax.named_scope("gather"):
        received = lax.all_to_all(mine, "band", 0, 0, axis_index_groups=rings, tiled=True)

    spectrum = call(
        forward_kernel, (length * 2 * 2 * planes, LANES), [vmem()] * 5, flops, "forward_zy"
    )(orbitals, other, received, left, right)
    with jax.named_scope("to_columns"):
        spectrum = lax.all_to_all(
            spectrum.reshape(columns, rows * 2 * 2 * planes, LANES), "fft", 0, 0, tiled=True
        )
    with jax.named_scope("swap_received"):
        received_other = lax.ppermute(received, "band", swap)
    spectrum = call(
        middle_kernel,
        (2, columns, rows, 2 * planes, LANES),
        [vmem()] * 4,
        flops,
        "solve_x",
        out_specs=pl.BlockSpec(memory_space=pl.ANY),
        scratch_shapes=[
            pltpu.VMEM((2, columns, rows, 2 * planes, LANES), jnp.float32),
            pltpu.SemaphoreType.DMA((2, SHARES)),
        ],
    )(table, spectrum.reshape(columns, rows, 2, 2 * planes, LANES), x_forward, x_backward)
    sharing = [
        [(a * ring + y) * columns + f for a in range(2) for f in range(columns)] for y in range(ring)
    ]
    with jax.named_scope("to_planes"):
        spectrum = lax.all_to_all(
            spectrum.reshape(2 * columns, rows * 2 * planes, LANES),
            ("band", "fft"),
            0,
            0,
            axis_index_groups=sharing,
            tiled=True,
        )
    return call(
        backward_kernel,
        orbitals.shape,
        [vmem()] * 5,
        flops,
        "backward_yz",
        out_specs=pl.BlockSpec(memory_space=pl.ANY),
        scratch_shapes=[
            pltpu.VMEM(orbitals.shape, jnp.float32),
            pltpu.SemaphoreType.DMA((bands, planes)),
        ],
    )(
        spectrum.reshape(2, columns * rows * 2 * planes, LANES),
        received,
        received_other,
        right,
        left,
    )


def solution(mesh):
    return jax.shard_map(
        body,
        mesh=mesh,
        in_specs=(P("band", "fft", None, None), P(), P()),
        out_specs=P("band", "fft", None, None),
        check_vma=False,
    )
```

```python
import math

import jax
import jax.numpy as jnp
import numpy as np
from jax import lax
from jax.experimental import pallas as pl
from jax.experimental.pallas import tpu as pltpu
from jax.sharding import PartitionSpec as P

SCREEN = 0.025
FRACTION = 0.25
LANES = 128
BATCH = 2
RING = 8
PLACES = (0, 4, 2, 6, 1, 5, 3, 7)
PLANES = 4
MATRICES = 4
VMEM_LIMIT = 40 * 1024 * 1024


def wave_matrix(length):
    indices = np.arange(length)
    angles = (indices[:, None] * indices[None, :] % length) * (2.0 * math.pi / length)
    cosine, sine = np.cos(angles), np.sin(angles)
    return np.block([[cosine, sine], [-sine, cosine]]).astype(np.float32)


def split(value):
    high = value.astype(jnp.bfloat16)
    low = (value - high.astype(jnp.float32)).astype(jnp.bfloat16)
    return high, low


def dot(left, right):
    return jnp.dot(left, right, preferred_element_type=jnp.float32)


def left_product(matrix, value):
    high, low = split(value)
    return dot(matrix[0], high) + (dot(matrix[0], low) + dot(matrix[1], high))


def right_product(value, matrix):
    high, low = split(value)
    return dot(high, matrix[0]) + (dot(low, matrix[0]) + dot(high, matrix[1]))


def prepare_kernel(owner, occupied, *refs):
    matrices, (leader, *parts, table) = refs[:MATRICES], refs[MATRICES:]
    leader[...] = jnp.broadcast_to(owner[:, :1].astype(jnp.float32), leader.shape)
    for matrix, part in zip(matrices, parts):
        part[0], part[1] = split(matrix[...])
    ring = lax.axis_index("band") // RING
    group = lax.broadcasted_iota(jnp.int32, occupied.shape, 1)
    named = (group == owner[:, :1]) & (occupied[...] == ring)
    count = jnp.sum(jnp.where(named, 1.0, 0.0), axis=(0, 1), keepdims=True)
    rows, size, lanes = table.shape
    length = size // 2
    planes = length // lax.axis_size("fft")
    row = lax.broadcasted_iota(jnp.int32, (size, lanes), 0)
    wave_x = signed_wave((row // (2 * planes)) * planes + row % planes, length)
    wave_z = signed_wave(lax.broadcasted_iota(jnp.int32, (size, lanes), 1), length)
    flat = wave_x * wave_x + wave_z * wave_z + SCREEN
    factor = count * (-FRACTION * 4.0 * math.pi / float(length**3))
    for k in range(rows):
        wave_y = signed_wave(lax.axis_index("fft") * rows + k, length)
        table[k] = factor / (flat + wave_y * wave_y)


def spread_kernel(leader, pieces, out):
    shape = pieces.shape[1:]
    chosen = jnp.broadcast_to(leader[:1], shape)
    piece = jnp.zeros(shape, jnp.float32)
    for k in range(pieces.shape[0]):
        piece = jnp.where(chosen == float(k), pieces[k], piece)
    for k in range(out.shape[0]):
        out[k] = piece


def tile(value, row, column, size):
    return value[row * size : (row + 1) * size, column * size : (column + 1) * size]


def plane(received, p):
    pieces = len(PLACES) // (received.shape[0] * received.shape[1] // LANES)
    return jnp.concatenate(
        [received[PLACES.index(p * pieces + k)] for k in range(pieces)], axis=0
    )


def forward_kernel(own, other, received, left, right, out, result, done):
    planes, length = own.shape[1], own.shape[2]
    columns, _, rows, lanes = out.shape
    copies = []
    for s, orbitals in enumerate((own, other)):
        for first in range(0, planes, BATCH):
            group = range(first, first + BATCH)
            fields = []
            for p in group:
                partner = plane(received, p)
                fields.append(jnp.concatenate([orbitals[c, p] * partner for c in range(2)], axis=1))
            along_z = right_product(jnp.concatenate(fields, axis=0), right)
            blocks = [
                jnp.concatenate([tile(along_z, k, c, length) for k in range(BATCH)], axis=1)
                for c in range(2)
            ]
            both = left_product(left, jnp.concatenate(blocks, axis=0))
            for k, p in enumerate(group):
                for c in range(2):
                    place = pl.ds(c * planes + p, length, stride=2 * planes)
                    result[s, place, :] = tile(both, c, k, length)
        field = result.at[s].reshape(columns, rows, lanes)
        copies.append(pltpu.make_async_copy(field, out.at[:, s], done.at[s]))
        copies[-1].start()
    for copy in copies:
        copy.wait()


def signed_wave(index, length):
    signed = jnp.where(index <= length // 2, index, index - length)
    return signed.astype(jnp.float32) * (2.0 * math.pi / length)


def middle_kernel(table, field, forward, backward, received, out):
    sources, fields, rows, parts, lanes = field.shape
    size = sources * parts
    ring = lax.axis_index("band") // RING
    items = [(k, s) for k in range(rows) for s in range(fields)]
    value = jnp.concatenate([field[:, s, k].reshape(size, lanes) for k, s in items], axis=1)
    kernels = jnp.concatenate([table[k] for k, _ in items], axis=1)
    value = left_product(backward, left_product(forward, value) * kernels)
    for n, (k, s) in enumerate(items):
        target = ring if s == 0 else 1 - ring
        block = value[:, n * lanes : (n + 1) * lanes]
        out[target, :, k] = block.reshape(sources, parts, lanes)


def backward_kernel(field, own, other, left, right, out, result, done):
    planes, length = result.shape[1], result.shape[2]
    ring = lax.axis_index("band") // RING
    partners = ((ring, own), (1 - ring, other))
    copies = []
    for first in range(0, planes, PLANES):
        group = range(first, first + PLANES)
        blocks = []
        for c in range(2):
            rows = [pl.ds(c * planes + p, length, stride=2 * planes) for p in group]
            blocks.append(
                jnp.concatenate([field[j, row, :] for row in rows for j, _ in partners], axis=1)
            )
        along_y = left_product(left, jnp.concatenate(blocks, axis=0))
        wide = [
            jnp.concatenate([tile(along_y, c, k, length) for c in range(2)], axis=1)
            for k in range(PLANES * len(partners))
        ]
        both = right_product(jnp.concatenate(wide, axis=0), right)
        for n, p in enumerate(group):
            for c in range(2):
                result[c, p] = sum(
                    tile(both, n * len(partners) + k, c, length) * plane(partner, p)
                    for k, (_, partner) in enumerate(partners)
                )
                copies.append(pltpu.make_async_copy(result.at[c, p], out.at[c, p], done.at[c, p]))
                copies[-1].start()
    for copy in copies:
        copy.wait()


def vmem():
    return pl.BlockSpec(memory_space=pltpu.VMEM)


def call(kernel, shape, specs, flops, name, types=jnp.float32, **options):
    options.setdefault("out_specs", vmem())
    if isinstance(shape, list):
        out_shape = [jax.ShapeDtypeStruct(s, t) for s, t in zip(shape, types)]
    else:
        out_shape = jax.ShapeDtypeStruct(shape, types)
    return pl.pallas_call(
        kernel,
        out_shape=out_shape,
        in_specs=specs,
        compiler_params=pltpu.CompilerParams(vmem_limit_bytes=VMEM_LIMIT),
        cost_estimate=pl.CostEstimate(flops=flops, bytes_accessed=4 << 20, transcendentals=0),
        name=name,
        **options,
    )


def body(orbitals, owner, occupied):
    bands, planes, length, _ = orbitals.shape
    groups = lax.axis_size("band")
    columns = lax.axis_size("fft")
    rows = length // columns
    ring = RING
    order = occupied.T
    flops = 2 * 2 * 3 * 2 * (2 * length) * (2 * length) * planes * length

    swap = [(k, (k + ring) % groups) for k in range(groups)]
    with jax.named_scope("swap_orbitals"):
        other = lax.ppermute(orbitals, "band", swap)

    with jax.named_scope("scatter"):
        pieces = lax.all_to_all(orbitals.reshape(groups, -1, LANES), "band", 0, 0, tiled=True)
    matrix = wave_matrix(length)
    x_index = np.arange(length).reshape(columns, 1, planes) + np.array([0, length])[None, :, None]
    x_index = x_index.reshape(-1)
    mixed = matrix[np.ix_(x_index, x_index)]
    leader, left, right, x_forward, x_backward, table = call(
        prepare_kernel,
        [(8, LANES)] + [(2, 2 * length, 2 * length)] * MATRICES + [(rows, 2 * length, LANES)],
        [vmem()] * (2 + MATRICES),
        flops,
        "prepare",
        types=[jnp.float32] + [jnp.bfloat16] * MATRICES + [jnp.float32],
        out_specs=[vmem()] * (2 + MATRICES),
    )(owner.reshape(1, -1), order, matrix, matrix.T.copy(), mixed, mixed.T.copy())
    mine = call(spread_kernel, (ring,) + pieces.shape[1:], [vmem()] * 2, 0, "spread")(leader, pieces)
    rings = [[a * ring + y for y in PLACES] for a in range(2)]
    with jax.named_scope("gather"):
        received = lax.all_to_all(mine, "band", 0, 0, axis_index_groups=rings, tiled=True)

    shape = (columns, 2, rows * 2 * planes, LANES)
    spectrum = call(
        forward_kernel,
        shape,
        [vmem()] * 5,
        flops,
        "forward_zy",
        out_specs=pl.BlockSpec(memory_space=pl.ANY),
        scratch_shapes=[
            pltpu.VMEM((2, length * 2 * planes, LANES), jnp.float32),
            pltpu.SemaphoreType.DMA((2,)),
        ],
    )(orbitals, other, received, left, right)
    with jax.named_scope("to_columns"):
        spectrum = lax.all_to_all(
            spectrum.reshape(columns, rows * 2 * 2 * planes, LANES), "fft", 0, 0, tiled=True
        )
    with jax.named_scope("swap_received"):
        received_other = lax.ppermute(received, "band", swap)
    spectrum = call(
        middle_kernel,
        (2, columns, rows, 2 * planes, LANES),
        [vmem()] * 4 + [pl.BlockSpec(memory_space=pl.ANY)],
        flops,
        "solve_x",
    )(
        table,
        spectrum.reshape(columns, 2, rows, 2 * planes, LANES),
        x_forward,
        x_backward,
        received_other,
    )
    sharing = [
        [(a * ring + y) * columns + f for a in range(2) for f in range(columns)] for y in range(ring)
    ]
    with jax.named_scope("to_planes"):
        spectrum = lax.all_to_all(
            spectrum.reshape(2 * columns, rows * 2 * planes, LANES),
            ("band", "fft"),
            0,
            0,
            axis_index_groups=sharing,
            tiled=True,
        )
    return call(
        backward_kernel,
        orbitals.shape,
        [vmem()] * 5,
        flops,
        "backward_yz",
        out_specs=pl.BlockSpec(memory_space=pl.ANY),
        scratch_shapes=[
            pltpu.VMEM(orbitals.shape, jnp.float32),
            pltpu.SemaphoreType.DMA((bands, planes)),
        ],
    )(
        spectrum.reshape(2, columns * rows * 2 * planes, LANES),
        received,
        received_other,
        right,
        left,
    )


def solution(mesh):
    return jax.shard_map(
        body,
        mesh=mesh,
        in_specs=(P("band", "fft", None, None), P(), P()),
        out_specs=P("band", "fft", None, None),
        check_vma=False,
    )
```

```python
import math

import jax
import jax.numpy as jnp
import numpy as np
from jax import lax
from jax.experimental import pallas as pl
from jax.experimental.pallas import tpu as pltpu
from jax.sharding import PartitionSpec as P

SCREEN = 0.025
FRACTION = 0.25
LANES = 128
BATCH = 2
RING = 8
PLACES = (0, 4, 2, 6, 3, 7, 1, 5)
PLANES = 4
MATRICES = 4
VMEM_LIMIT = 40 * 1024 * 1024


def wave_matrix(length):
    indices = np.arange(length)
    angles = (indices[:, None] * indices[None, :] % length) * (2.0 * math.pi / length)
    cosine, sine = np.cos(angles), np.sin(angles)
    return np.block([[cosine, sine], [-sine, cosine]]).astype(np.float32)


def split(value):
    high = value.astype(jnp.bfloat16)
    low = (value - high.astype(jnp.float32)).astype(jnp.bfloat16)
    return high, low


def dot(left, right):
    return jnp.dot(left, right, preferred_element_type=jnp.float32)


def left_product(matrix, value):
    high, low = split(value)
    return dot(matrix[0], high) + (dot(matrix[0], low) + dot(matrix[1], high))


def right_product(value, matrix):
    high, low = split(value)
    return dot(high, matrix[0]) + (dot(low, matrix[0]) + dot(high, matrix[1]))


def prepare_kernel(owner, occupied, *refs):
    matrices, (leader, *parts, table) = refs[:MATRICES], refs[MATRICES:]
    leader[...] = jnp.broadcast_to(owner[:, :1].astype(jnp.float32), leader.shape)
    for matrix, part in zip(matrices, parts):
        part[0], part[1] = split(matrix[...])
    ring = lax.axis_index("band") // RING
    group = lax.broadcasted_iota(jnp.int32, occupied.shape, 1)
    named = (group == owner[:, :1]) & (occupied[...] == ring)
    count = jnp.sum(jnp.where(named, 1.0, 0.0), axis=(0, 1), keepdims=True)
    rows, size, lanes = table.shape
    length = size // 2
    planes = length // lax.axis_size("fft")
    row = lax.broadcasted_iota(jnp.int32, (size, lanes), 0)
    wave_x = signed_wave((row // (2 * planes)) * planes + row % planes, length)
    wave_z = signed_wave(lax.broadcasted_iota(jnp.int32, (size, lanes), 1), length)
    flat = wave_x * wave_x + wave_z * wave_z + SCREEN
    factor = count * (-FRACTION * 4.0 * math.pi / float(length**3))
    for k in range(rows):
        wave_y = signed_wave(lax.axis_index("fft") * rows + k, length)
        table[k] = factor / (flat + wave_y * wave_y)


def spread_kernel(leader, pieces, out):
    shape = pieces.shape[1:]
    chosen = jnp.broadcast_to(leader[:1], shape)
    piece = jnp.zeros(shape, jnp.float32)
    for k in range(pieces.shape[0]):
        piece = jnp.where(chosen == float(k), pieces[k], piece)
    for k in range(out.shape[0]):
        out[k] = piece


def tile(value, row, column, size):
    return value[row * size : (row + 1) * size, column * size : (column + 1) * size]


def plane(received, p):
    pieces = len(PLACES) // (received.shape[0] * received.shape[1] // LANES)
    return jnp.concatenate(
        [received[PLACES.index(p * pieces + k)] for k in range(pieces)], axis=0
    )


def forward_kernel(own, other, received, left, right, out, result, done):
    planes, length = own.shape[1], own.shape[2]
    columns, _, rows, lanes = out.shape
    copies = []
    for s, orbitals in enumerate((own, other)):
        for first in range(0, planes, BATCH):
            group = range(first, first + BATCH)
            fields = []
            for p in group:
                partner = plane(received, p)
                fields.append(jnp.concatenate([orbitals[c, p] * partner for c in range(2)], axis=1))
            along_z = right_product(jnp.concatenate(fields, axis=0), right)
            blocks = [
                jnp.concatenate([tile(along_z, k, c, length) for k in range(BATCH)], axis=1)
                for c in range(2)
            ]
            both = left_product(left, jnp.concatenate(blocks, axis=0))
            for k, p in enumerate(group):
                for c in range(2):
                    place = pl.ds(c * planes + p, length, stride=2 * planes)
                    result[s, place, :] = tile(both, c, k, length)
        field = result.at[s].reshape(columns, rows, lanes)
        copies.append(pltpu.make_async_copy(field, out.at[:, s], done.at[s]))
        copies[-1].start()
    for copy in copies:
        copy.wait()


def signed_wave(index, length):
    signed = jnp.where(index <= length // 2, index, index - length)
    return signed.astype(jnp.float32) * (2.0 * math.pi / length)


def middle_kernel(table, field, forward, backward, received, out):
    sources, fields, rows, parts, lanes = field.shape
    size = sources * parts
    ring = lax.axis_index("band") // RING
    items = [(k, s) for k in range(rows) for s in range(fields)]
    value = jnp.concatenate([field[:, s, k].reshape(size, lanes) for k, s in items], axis=1)
    kernels = jnp.concatenate([table[k] for k, _ in items], axis=1)
    value = left_product(backward, left_product(forward, value) * kernels)
    for n, (k, s) in enumerate(items):
        target = ring if s == 0 else 1 - ring
        block = value[:, n * lanes : (n + 1) * lanes]
        out[target, :, k] = block.reshape(sources, parts, lanes)


def backward_kernel(field, own, other, left, right, out, result, done):
    planes, length = result.shape[1], result.shape[2]
    ring = lax.axis_index("band") // RING
    partners = ((ring, own), (1 - ring, other))
    copies = []
    for first in range(0, planes, PLANES):
        group = range(first, first + PLANES)
        blocks = []
        for c in range(2):
            rows = [pl.ds(c * planes + p, length, stride=2 * planes) for p in group]
            blocks.append(
                jnp.concatenate([field[j, row, :] for row in rows for j, _ in partners], axis=1)
            )
        along_y = left_product(left, jnp.concatenate(blocks, axis=0))
        wide = [
            jnp.concatenate([tile(along_y, c, k, length) for c in range(2)], axis=1)
            for k in range(PLANES * len(partners))
        ]
        both = right_product(jnp.concatenate(wide, axis=0), right)
        for n, p in enumerate(group):
            for c in range(2):
                result[c, p] = sum(
                    tile(both, n * len(partners) + k, c, length) * plane(partner, p)
                    for k, (_, partner) in enumerate(partners)
                )
                copies.append(pltpu.make_async_copy(result.at[c, p], out.at[c, p], done.at[c, p]))
                copies[-1].start()
    for copy in copies:
        copy.wait()


def vmem():
    return pl.BlockSpec(memory_space=pltpu.VMEM)


def call(kernel, shape, specs, flops, name, types=jnp.float32, **options):
    options.setdefault("out_specs", vmem())
    if isinstance(shape, list):
        out_shape = [jax.ShapeDtypeStruct(s, t) for s, t in zip(shape, types)]
    else:
        out_shape = jax.ShapeDtypeStruct(shape, types)
    return pl.pallas_call(
        kernel,
        out_shape=out_shape,
        in_specs=specs,
        compiler_params=pltpu.CompilerParams(vmem_limit_bytes=VMEM_LIMIT),
        cost_estimate=pl.CostEstimate(flops=flops, bytes_accessed=4 << 20, transcendentals=0),
        name=name,
        **options,
    )


def body(orbitals, owner, occupied):
    bands, planes, length, _ = orbitals.shape
    groups = lax.axis_size("band")
    columns = lax.axis_size("fft")
    rows = length // columns
    ring = RING
    order = occupied.T
    flops = 2 * 2 * 3 * 2 * (2 * length) * (2 * length) * planes * length

    swap = [(k, (k + ring) % groups) for k in range(groups)]
    with jax.named_scope("swap_orbitals"):
        other = lax.ppermute(orbitals, "band", swap)

    with jax.named_scope("scatter"):
        pieces = lax.all_to_all(orbitals.reshape(groups, -1, LANES), "band", 0, 0, tiled=True)
    matrix = wave_matrix(length)
    x_index = np.arange(length).reshape(columns, 1, planes) + np.array([0, length])[None, :, None]
    x_index = x_index.reshape(-1)
    mixed = matrix[np.ix_(x_index, x_index)]
    leader, left, right, x_forward, x_backward, table = call(
        prepare_kernel,
        [(8, LANES)] + [(2, 2 * length, 2 * length)] * MATRICES + [(rows, 2 * length, LANES)],
        [vmem()] * (2 + MATRICES),
        flops,
        "prepare",
        types=[jnp.float32] + [jnp.bfloat16] * MATRICES + [jnp.float32],
        out_specs=[vmem()] * (2 + MATRICES),
    )(owner.reshape(1, -1), order, matrix, matrix.T.copy(), mixed, mixed.T.copy())
    mine = call(spread_kernel, (ring,) + pieces.shape[1:], [vmem()] * 2, 0, "spread")(leader, pieces)
    rings = [[a * ring + y for y in PLACES] for a in range(2)]
    with jax.named_scope("gather"):
        received = lax.all_to_all(mine, "band", 0, 0, axis_index_groups=rings, tiled=True)

    shape = (columns, 2, rows * 2 * planes, LANES)
    spectrum = call(
        forward_kernel,
        shape,
        [vmem()] * 5,
        flops,
        "forward_zy",
        out_specs=pl.BlockSpec(memory_space=pl.ANY),
        scratch_shapes=[
            pltpu.VMEM((2, length * 2 * planes, LANES), jnp.float32),
            pltpu.SemaphoreType.DMA((2,)),
        ],
    )(orbitals, other, received, left, right)
    with jax.named_scope("to_columns"):
        spectrum = lax.all_to_all(
            spectrum.reshape(columns, rows * 2 * 2 * planes, LANES), "fft", 0, 0, tiled=True
        )
    with jax.named_scope("swap_received"):
        received_other = lax.ppermute(received, "band", swap)
    spectrum = call(
        middle_kernel,
        (2, columns, rows, 2 * planes, LANES),
        [vmem()] * 4 + [pl.BlockSpec(memory_space=pl.ANY)],
        flops,
        "solve_x",
    )(
        table,
        spectrum.reshape(columns, 2, rows, 2 * planes, LANES),
        x_forward,
        x_backward,
        received_other,
    )
    sharing = [
        [(a * ring + y) * columns + f for a in range(2) for f in range(columns)] for y in range(ring)
    ]
    with jax.named_scope("to_planes"):
        spectrum = lax.all_to_all(
            spectrum.reshape(2 * columns, rows * 2 * planes, LANES),
            ("band", "fft"),
            0,
            0,
            axis_index_groups=sharing,
            tiled=True,
        )
    return call(
        backward_kernel,
        orbitals.shape,
        [vmem()] * 5,
        flops,
        "backward_yz",
        out_specs=pl.BlockSpec(memory_space=pl.ANY),
        scratch_shapes=[
            pltpu.VMEM(orbitals.shape, jnp.float32),
            pltpu.SemaphoreType.DMA((bands, planes)),
        ],
    )(
        spectrum.reshape(2, columns * rows * 2 * planes, LANES),
        received,
        received_other,
        right,
        left,
    )


def solution(mesh):
    return jax.shard_map(
        body,
        mesh=mesh,
        in_specs=(P("band", "fft", None, None), P(), P()),
        out_specs=P("band", "fft", None, None),
        check_vma=False,
    )
```
